32 devices in a mesh: ctx: 8 (over z, y), head: 2 (over core), pair: 2 (over x).
Axes of the slice: x: 2, y: 2, z: 4, core: 2. Of those that a mesh axis runs over, the one named last changes fastest.
Arguments:
- tokens_in: bfloat16 [2, 256, 2048], P(None, ('ctx', 'pair')), may hold values from -6 to 6
- attn_gain: float32 [2048], replicated, may hold values from 0.1 to 1.9
- query_matrix: bfloat16 [2048, 2048], P(None, ('head', 'pair')), may hold values from -20 to 20
- key_matrix: bfloat16 [256, 2048], P(('head', 'pair')), may hold values from -1 to 1
- value_matrix: bfloat16 [256, 2048], P(('head', 'pair')), may hold values from -0.125 to 0.125
- output_matrix: bfloat16 [2048, 2048], P(None, ('head', 'pair')), may hold values from -0.125 to 0.125
- moe_gain: float32 [2048], replicated, may hold values from 0.1 to 1.9
- chosen_experts: int32 [2, 256, 8], P('head', ('ctx', 'pair')), may hold values from 0 to 15, all different within a row; in each aligned block of 16 rows (0 to 15, 16 to 31, ..., all dimensions but the last counted through in order) at most 9 rows name the same one
- combine_weights: float32 [2, 256, 8], P('head', ('ctx', 'pair')), may hold values from 0.02 to 0.5
- gate_weight: bfloat16 [16, 768, 2048], P(('ctx', 'head'), 'pair'), may hold values from -0.125 to 0.125
- up_weight: bfloat16 [16, 768, 2048], P(('ctx', 'head'), 'pair'), may hold values from -0.125 to 0.125
- down_weight: bfloat16 [16, 768, 2048], P(('ctx', 'head'), 'pair'), may hold values from -0.21875 to 0.21875
Outputs:
- layer_out: bfloat16 [2, 256, 2048], P('head', ('ctx', 'pair'))
The draws below stay inside these ranges and needn't reach their ends.
Inputs may be any that keep to these rules, and one draw needn't show every extreme that they name: `chosen_experts`: each token names 8 different experts; among the 16 tokens of one sequence that one device holds, no expert is named more than 9 times.
All inputs are finite; a program needn't handle non-finite values.
Results may differ from the reference program's by a relative error of at most 0.013.
Values may be sent and summed in bfloat16 or wider, within the bound.
A program may use at most 64 MiB of HBM per device.

```python
import math
import jax
import jax.numpy as jnp
import numpy as np
from jax import lax

MODEL_DIM = 2048
QUERY_HEADS = 16
KEY_VALUE_HEADS = 2
HEAD_SIZE = 128
FF = 768
TOP = 8
LEN_DEV = 16
SEQUENCE_COUNT = 2
SEQ_LENGTH = 256
EXPERTS = 16
CAP = 9
N_PAIR = 2


def shared_key_rows(key):
    sampled_values = jax.random.normal(jax.random.fold_in(key, 17), (MODEL_DIM, KEY_VALUE_HEADS * HEAD_SIZE), jnp.float32)
    return jnp.clip(sampled_values, -6.0, 6.0) / jnp.sqrt(jnp.float32(MODEL_DIM))


def draw_key_matrix(key, part):
    return shared_key_rows(key).T.astype(jnp.bfloat16)


def draw_query_matrix(key, part):
    sampled_values = jax.random.normal(jax.random.fold_in(key, 29), (MODEL_DIM, QUERY_HEADS, HEAD_SIZE), jnp.float32)
    matrix_out = jnp.clip(sampled_values, -6.0, 6.0) / jnp.sqrt(jnp.float32(MODEL_DIM))
    return matrix_out.reshape(MODEL_DIM, QUERY_HEADS * HEAD_SIZE).astype(jnp.bfloat16)


def block_scale(stream_key, shape, split, smallest, top_value):
    def one(axis_at, parts):
        draws = jax.random.uniform(jax.random.fold_in(jax.random.fold_in(stream_key, 6), axis_at), (parts,), jnp.float32, smallest / len(split), top_value / len(split))
        return jnp.repeat(jnp.exp(draws), shape[axis_at] // parts).reshape((-1,) + (1,) * (len(shape) - axis_at - 1))

    level = one(*split[0])
    for cut in split[1:]:
        level = level * one(*cut)
    return level


def deal_out(own_key, own, number, rows, amount, top, most, skew):
    sequence = jax.random.permutation(own_key, amount)
    heavy_load, usual = load_shares(amount, rows * top, most, skew, True), load_shares(amount, rows * top, most, skew, False)
    places = jnp.arange(amount)

    def named(tallies, rotation):
        used = int((tallies > 0).sum())
        fixed = max(1, used // 4)
        passed = fixed + (places - fixed + rotation * (used - fixed)) % max(1, amount - fixed)
        return jnp.zeros((amount,), jnp.int32).at[sequence[jnp.where(places < fixed, places, passed)]].set(jnp.asarray(tallies, jnp.int32))

    tallies = jnp.where(number % 4 == 0, named(heavy_load, number // 4), named(usual, number - number // 4 - 1))
    mixed = jax.random.permutation(jax.random.fold_in(own, 3), amount)
    giver, taker = mixed[0:amount // 2 * 2:2], mixed[1:amount // 2 * 2:2]
    room = jnp.minimum(tallies[giver] - 1, most - tallies[taker]) // 2
    room = jnp.where((giver == sequence[0]) | (taker == sequence[0]) | (tallies[taker] == 0), 0, jnp.maximum(room, 0))
    passed = jax.random.randint(jax.random.fold_in(own, 4), (amount // 2,), 0, 1 << 20) % (room + 1)
    tallies = tallies.at[giver].add(-passed).at[taker].add(passed)
    items = jnp.searchsorted(jnp.cumsum(tallies), jnp.arange(rows * top), side="right").astype(jnp.int32)
    listing = items.reshape(top, rows).T
    listing = listing[jax.random.permutation(jax.random.fold_in(own, 1), rows)]
    rotation = jax.random.randint(jax.random.fold_in(own, 2), (rows, 1), 0, top)
    return jnp.take_along_axis(listing, (jnp.arange(top)[None, :] + rotation) % top, axis=1)


def load_shares(count, total, bound, skew, full):
    portions = [(1 << 20) // math.isqrt(grade ** skew) + 1 for grade in range(1, count + 1)]
    largest = bound if full else min(bound, max(-(-total // count), total * portions[0] // sum(portions)))
    least = 1 if total - largest >= count - 1 else 0
    counts, rest = [largest] + [least] * (count - 1), total - largest - least * (count - 1)
    while rest > 0:
        candidates = [i for i in range(1, count) if counts[i] < largest] or [i for i in range(1, count) if counts[i] < bound]
        whole, remaining = sum([portions[i] for i in candidates]), rest
        for i in candidates:
            more = min(bound - counts[i], max(1, remaining * portions[i] // whole), rest)
            counts[i] = counts[i] + more
            rest = rest - more
    return np.array(counts)


def noise(rng, extent, deviation, bound, pieces=(), dtype=jnp.bfloat16):
    entries = jax.random.normal(rng, extent, jnp.float32) * deviation
    if len(pieces) > 0:
        entries = block_scale(rng, extent, pieces, -0.22, 0.18) * entries
    return jnp.clip(entries, min=-bound, max=bound).astype(dtype)


def setup_inputs(seed: int = 0) -> dict:
    key_list = jax.random.split(jax.random.key(seed), 13)
    tokens_in = noise(key_list[0], (SEQUENCE_COUNT, SEQ_LENGTH, MODEL_DIM), 1.0, 6.0, ((1, 16),))
    attn_gain = jnp.clip(1.0 + 0.18 * jax.random.normal(key_list[1], (MODEL_DIM,), jnp.float32), 0.1, 1.9)
    query_matrix = draw_query_matrix(jax.random.fold_in(key_list[12], 71), 0)
    key_matrix = draw_key_matrix(jax.random.fold_in(key_list[12], 71), 0)
    value_matrix = noise(key_list[4], (KEY_VALUE_HEADS * HEAD_SIZE, MODEL_DIM), MODEL_DIM ** -0.5, 0.125, ((0, 4),))
    output_matrix = noise(key_list[5], (QUERY_HEADS * HEAD_SIZE, MODEL_DIM), (QUERY_HEADS * HEAD_SIZE) ** -0.5, 0.125, ((1, 4),))
    moe_gain = jnp.clip(1.0 + 0.18 * jax.random.normal(key_list[6], (MODEL_DIM,), jnp.float32), 0.1, 1.9)
    chosen_experts_keys = jax.random.split(jax.random.fold_in(key_list[7], 1), SEQUENCE_COUNT * SEQ_LENGTH // LEN_DEV)
    chosen_experts_turns = jax.random.permutation(jax.random.fold_in(key_list[7], 3), SEQUENCE_COUNT * SEQ_LENGTH // LEN_DEV)
    chosen_experts = jax.vmap(lambda own, number: deal_out(jax.random.fold_in(key_list[7], 2), own, number, LEN_DEV, EXPERTS, TOP, CAP, 0))(chosen_experts_keys, chosen_experts_turns).reshape((SEQUENCE_COUNT, SEQ_LENGTH, TOP))
    combine_weights = jnp.clip(jnp.exp(math.log(0.5) - 3.218876 * jax.random.uniform(key_list[8], (SEQUENCE_COUNT, SEQ_LENGTH, TOP), jnp.float32) ** block_scale(key_list[8], (SEQUENCE_COUNT, SEQ_LENGTH, TOP), ((0, 2), (1, 16)), -0.2, 0.2)), 0.02, 0.5)
    gate_weight = noise(key_list[9], (EXPERTS, FF, MODEL_DIM), MODEL_DIM ** -0.5, 0.125, ((0, 16), (1, 2)))
    up_weight = noise(key_list[10], (EXPERTS, FF, MODEL_DIM), MODEL_DIM ** -0.5, 0.125, ((0, 16), (1, 2)))
    down_weight = noise(key_list[11], (EXPERTS, FF, MODEL_DIM), FF ** -0.5, 0.21875, ((0, 16), (1, 2)))
    return dict(tokens_in=tokens_in, attn_gain=attn_gain, query_matrix=query_matrix, key_matrix=key_matrix, value_matrix=value_matrix, output_matrix=output_matrix, moe_gain=moe_gain, chosen_experts=chosen_experts, combine_weights=combine_weights, gate_weight=gate_weight, up_weight=up_weight, down_weight=down_weight)


ROPE_BASE = 1000000.0
EPSILON = 1e-06

def normalize(values, gain_vector):
    wide = values.astype(jnp.float32)
    mean_square = lax.optimization_barrier(jnp.mean(wide * wide, axis=-1, keepdims=True))
    return (wide * lax.rsqrt(mean_square + EPSILON) * gain_vector).astype(jnp.bfloat16)

def rotate(values, positions):
    half_dim = values.shape[-1] // 2
    frequency = ROPE_BASE ** (-(jnp.arange(half_dim).astype(jnp.float32) * 2.0) / values.shape[-1])
    angles = positions[:, None] * frequency[None, :]
    cosine_part = jnp.cos(angles)[:, None, :]
    sine_part = jnp.sin(angles)[:, None, :]
    lower_half = values[..., :half_dim]
    upper_half = values[..., half_dim:]
    return jnp.concatenate([lower_half * cosine_part - upper_half * sine_part, upper_half * cosine_part + lower_half * sine_part], axis=-1)

def reference(tokens_in, attn_gain, query_matrix, key_matrix, value_matrix, output_matrix, moe_gain, chosen_experts, combine_weights, gate_weight, up_weight, down_weight):
    normalized_input = normalize(tokens_in, attn_gain).astype(jnp.float32)
    positions = jnp.arange(SEQ_LENGTH).astype(jnp.float32)
    query_unrotated = jnp.einsum('ynx,xq->ynq', normalized_input, query_matrix.astype(jnp.float32)).reshape(SEQUENCE_COUNT, SEQ_LENGTH, QUERY_HEADS, HEAD_SIZE)
    queries = rotate(query_unrotated, positions).astype(jnp.bfloat16)
    key_unrotated = jnp.einsum('mzr,tr->mzt', normalized_input, key_matrix.astype(jnp.float32)).reshape(SEQUENCE_COUNT, SEQ_LENGTH, KEY_VALUE_HEADS, HEAD_SIZE)
    rotated_keys = rotate(key_unrotated, positions).astype(jnp.bfloat16)
    every_value_row = jnp.einsum('mzr,tr->mzt', normalized_input, value_matrix.astype(jnp.float32)).reshape(SEQUENCE_COUNT, SEQ_LENGTH, KEY_VALUE_HEADS, HEAD_SIZE).astype(jnp.bfloat16)
    group_width = QUERY_HEADS // KEY_VALUE_HEADS
    scaling = HEAD_SIZE ** (-0.5)
    causal = jnp.arange(SEQ_LENGTH)[None, :] <= jnp.arange(SEQ_LENGTH)[:, None]

    def attend(pair_id):
        seq_id = pair_id // QUERY_HEADS
        head_id = pair_id % QUERY_HEADS
        query_rows = queries[seq_id, :, head_id]
        key_rows = rotated_keys[seq_id, :, head_id // group_width]
        value_rows = every_value_row[seq_id, :, head_id // group_width]
        scores = jnp.dot(query_rows, key_rows.T, preferred_element_type=jnp.float32) * scaling
        scores = jnp.where(causal, scores, -1e+30)
        row_peak = lax.optimization_barrier(jnp.max(scores, axis=-1, keepdims=True))
        weights = jnp.where(causal, jnp.exp(scores - row_peak), 0.0)
        row_total = lax.optimization_barrier(jnp.sum(weights, axis=-1, keepdims=True))
        mixed = jnp.dot(weights.astype(jnp.bfloat16), value_rows, preferred_element_type=jnp.float32) / row_total
        return mixed.astype(jnp.bfloat16)
    head_results = lax.map(attend, jnp.arange(SEQUENCE_COUNT * QUERY_HEADS))
    head_results = head_results.reshape(SEQUENCE_COUNT, QUERY_HEADS, SEQ_LENGTH, HEAD_SIZE).transpose(0, 2, 1, 3).reshape(SEQUENCE_COUNT, SEQ_LENGTH, QUERY_HEADS * HEAD_SIZE)
    attention_output = jnp.einsum('kem,mv->kev', head_results.astype(jnp.float32), output_matrix.astype(jnp.float32)).astype(jnp.bfloat16)
    residual = (tokens_in.astype(jnp.float32) + attention_output.astype(jnp.float32)).astype(jnp.bfloat16)
    moe_in = normalize(residual, moe_gain).reshape(SEQUENCE_COUNT * SEQ_LENGTH, MODEL_DIM)
    flat_expert = chosen_experts.reshape(-1)
    flat_weight = combine_weights.reshape(-1)
    slot_count = CAP * (SEQUENCE_COUNT * SEQ_LENGTH // LEN_DEV)
    quarter = FF // N_PAIR

    def expert_step(totals, inputs):
        expert_id, gate_local, up_local, down_local = inputs
        matches = flat_expert == expert_id
        picked = jnp.nonzero(matches, size=slot_count, fill_value=0)[0].astype(jnp.int32)
        is_live = jnp.arange(slot_count) < jnp.sum(matches.astype(jnp.int32))
        token_ids = picked // TOP
        row_block = moe_in[token_ids]
        gate_part = lax.dot_general(row_block, gate_local, (((1,), (1,)), ((), ())), preferred_element_type=jnp.float32)
        up_part = lax.dot_general(row_block, up_local, (((1,), (1,)), ((), ())), preferred_element_type=jnp.float32)
        hidden = (jax.nn.silu(gate_part) * up_part).astype(jnp.bfloat16)
        output_sum = jnp.zeros((slot_count, MODEL_DIM), jnp.float32)
        for part_id in range(N_PAIR):
            lower_col = part_id * quarter
            partial_value = jnp.dot(hidden[:, lower_col:lower_col + quarter], down_local[lower_col:lower_col + quarter, :], preferred_element_type=jnp.float32)
            output_sum = output_sum + lax.optimization_barrier(partial_value.astype(jnp.bfloat16)).astype(jnp.float32)
        expert_out = lax.optimization_barrier(output_sum.astype(jnp.bfloat16)).astype(jnp.float32)
        scaled = jnp.where(is_live, flat_weight[picked], 0.0)[:, None] * expert_out
        return (totals.at[token_ids].add(scaled), None)
    totals, unused = lax.scan(expert_step, jnp.zeros((SEQUENCE_COUNT * SEQ_LENGTH, MODEL_DIM), jnp.float32), (jnp.arange(EXPERTS).astype(jnp.int32), gate_weight, up_weight, down_weight))
    mixture = totals.reshape(SEQUENCE_COUNT, SEQ_LENGTH, MODEL_DIM)
    return (residual.astype(jnp.float32) + mixture).astype(jnp.bfloat16)
```

```python
import functools

import jax
import jax.numpy as jnp
import numpy as np
from jax import lax
from jax.experimental import pallas as pl
from jax.experimental.pallas import tpu as pltpu
from jax.sharding import PartitionSpec as P

ROPE_BASE = 1000000.0
EPSILON = 1e-06
MASKED = -1e30


def normalize(values, gain_vector):
    wide = values.astype(jnp.float32)
    mean_square = jnp.mean(wide * wide, axis=-1, keepdims=True)
    return (wide * lax.rsqrt(mean_square + EPSILON) * gain_vector).astype(jnp.bfloat16)


def rotate(values, positions):
    half_dim = values.shape[-1] // 2
    frequency = ROPE_BASE ** (-(jnp.arange(half_dim).astype(jnp.float32) * 2.0) / values.shape[-1])
    angles = positions[:, None] * frequency[None, :]
    cosine_part = jnp.cos(angles)[:, None, :]
    sine_part = jnp.sin(angles)[:, None, :]
    lower_half = values[..., :half_dim]
    upper_half = values[..., half_dim:]
    return jnp.concatenate(
        [
            lower_half * cosine_part - upper_half * sine_part,
            upper_half * cosine_part + lower_half * sine_part,
        ],
        axis=-1,
    )


def body(
    tokens_in,
    attn_gain,
    query_matrix,
    key_matrix,
    value_matrix,
    output_matrix,
    moe_gain,
    chosen_experts,
    combine_weights,
    gate_weight,
    up_weight,
    down_weight,
):
    pair_count = lax.axis_size("pair")
    head_count = lax.axis_size("head")
    ctx_count = lax.axis_size("ctx")
    seq_count, own_len, model_width = tokens_in.shape
    block_len = own_len * pair_count
    normalized_input = normalize(tokens_in, attn_gain)
    block_rows = lax.all_gather(normalized_input, "pair", axis=1, tiled=True)
    block_start = lax.axis_index("ctx") * block_len
    query_pos = block_start + jnp.arange(block_len)
    positions = query_pos.astype(jnp.float32)
    key_part = jnp.einsum("spd,hd->sph", block_rows, key_matrix, preferred_element_type=jnp.float32)
    value_part = jnp.einsum(
        "spd,hd->sph", block_rows, value_matrix, preferred_element_type=jnp.float32
    )
    key_full, value_full = (
        lax.all_gather(key_part.astype(jnp.bfloat16), "pair", axis=2, tiled=True).astype(
            key_part.dtype
        ),
        lax.all_gather(value_part.astype(jnp.bfloat16), "pair", axis=2, tiled=True).astype(
            value_part.dtype
        ),
    )
    head_dim = key_full.shape[2]
    local_heads = query_matrix.shape[1] // head_dim
    query_unrotated = jnp.einsum(
        "spd,dh->sph", block_rows, query_matrix, preferred_element_type=jnp.float32
    )
    queries = rotate(
        query_unrotated.reshape(seq_count, block_len, local_heads, head_dim), positions
    ).astype(jnp.bfloat16)
    rotated_keys = rotate(key_full.reshape(seq_count, block_len, 1, head_dim), positions)[
        :, :, 0
    ].astype(jnp.bfloat16)
    every_value_row = value_full.astype(jnp.bfloat16)
    scaling = head_dim ** (-0.5)
    last_query = block_start + block_len - 1
    start_state = (
        jnp.full((seq_count, block_len, local_heads), MASKED, jnp.float32),
        jnp.zeros((seq_count, block_len, local_heads), jnp.float32),
        jnp.zeros((seq_count, block_len, local_heads, head_dim), jnp.float32),
    )
    key_rows = lax.all_gather(rotated_keys, "ctx", axis=1, tiled=True)
    value_rows = lax.all_gather(every_value_row, "ctx", axis=1, tiled=True)
    key_span = key_rows.shape[1]

    def compute(running_state):
        row_peak, denominator, accumulated = running_state
        key_pos = jnp.arange(key_span)
        allowed = (key_pos[None, :] <= query_pos[:, None])[None, :, None, :]
        scores = (
            jnp.einsum("sphd,skd->sphk", queries, key_rows, preferred_element_type=jnp.float32)
            * scaling
        )
        scores = jnp.where(allowed, scores, MASKED)
        new_peak = jnp.maximum(row_peak, jnp.max(scores, axis=-1))
        weights = jnp.where(allowed, jnp.exp(scores - new_peak[..., None]), 0.0)
        denominator = jnp.sum(weights, axis=-1)
        accumulated = jnp.einsum(
            "sphk,skd->sphd",
            weights.astype(jnp.bfloat16),
            value_rows,
            preferred_element_type=jnp.float32,
        )
        return (new_peak, denominator, accumulated)

    row_peak, denominator, accumulated = lax.cond(
        jnp.int32(0) > last_query, lambda skipped: skipped, compute, start_state
    )
    attended = (
        (accumulated / denominator[..., None])
        .astype(jnp.bfloat16)
        .reshape(seq_count, block_len, local_heads * head_dim)
    )
    projected = jnp.einsum(
        "sph,hc->spc",
        lax.all_gather(attended, ("head", "pair"), axis=2, tiled=True),
        output_matrix,
        preferred_element_type=jnp.float32,
    )
    projected = projected.astype(jnp.bfloat16).reshape(
        seq_count * pair_count, own_len, output_matrix.shape[1]
    )
    owned_rows = lax.all_to_all(
        projected, ("head", "pair"), split_axis=0, concat_axis=2, tiled=True
    )[0]
    own_tokens = lax.dynamic_index_in_dim(tokens_in, lax.axis_index("head"), 0, keepdims=False)
    residual = (own_tokens.astype(jnp.float32) + owned_rows.astype(jnp.float32)).astype(
        jnp.bfloat16
    )
    moe_in = normalize(residual, moe_gain)
    expert_total = ctx_count * head_count
    top_count = chosen_experts.shape[-1]
    capacity = max(2, (own_len * top_count + expert_total - 1) // expert_total + 1)
    picked = chosen_experts.reshape(own_len, top_count)
    member = (picked[..., None] == jnp.arange(expert_total)[None, None, :]).astype(jnp.int32)
    flat_count = own_len * top_count
    earlier = jnp.tril(jnp.ones((flat_count, flat_count), jnp.bfloat16))
    running = (
        jnp.dot(
            earlier,
            member.reshape(flat_count, expert_total).astype(jnp.bfloat16),
            preferred_element_type=jnp.float32,
        )
        .astype(jnp.int32)
        .reshape(own_len, top_count, expert_total)
    )
    slot_rank = jnp.sum((running - 1) * member, axis=-1)
    slot_ids = picked * capacity + slot_rank
    placing = jnp.any(
        slot_ids[..., None] == jnp.arange(expert_total * capacity)[None, None, :], axis=1
    ).astype(jnp.bfloat16)
    outgoing = jnp.einsum("ts,td->sd", placing, moe_in, preferred_element_type=jnp.float32).astype(
        jnp.bfloat16
    )
    incoming = lax.all_to_all(
        outgoing.reshape(expert_total, capacity, model_width),
        ("ctx", "head"),
        split_axis=0,
        concat_axis=0,
        tiled=True,
    )
    incoming = incoming.reshape(expert_total * capacity, model_width)
    slot_rows = incoming.shape[0]
    gate_local = gate_weight[0]
    up_local = up_weight[0]
    down_local = down_weight[0]
    quarter = gate_local.shape[0]
    totals = jnp.zeros((slot_rows, model_width), jnp.float32)
    gate_rows_w = lax.all_gather(gate_local, "pair", axis=0, tiled=True)
    up_rows_w = lax.all_gather(up_local, "pair", axis=0, tiled=True)
    down_rows_w = lax.all_gather(down_local, "pair", axis=0, tiled=True)
    for part_id in range(gate_rows_w.shape[0] // quarter):
        lower_row = part_id * quarter
        gate_part = lax.dot_general(
            gate_rows_w[lower_row : lower_row + quarter],
            incoming,
            (((1,), (1,)), ((), ())),
            preferred_element_type=jnp.float32,
        )
        up_part = lax.dot_general(
            up_rows_w[lower_row : lower_row + quarter],
            incoming,
            (((1,), (1,)), ((), ())),
            preferred_element_type=jnp.float32,
        )
        hidden = (jax.nn.silu(gate_part) * up_part).astype(jnp.bfloat16)
        partial_value = lax.dot_general(
            hidden,
            down_rows_w[lower_row : lower_row + quarter],
            (((0,), (0,)), ((), ())),
            preferred_element_type=jnp.float32,
        )
        totals = totals + lax.optimization_barrier(partial_value.astype(jnp.bfloat16)).astype(
            jnp.float32
        )
    expert_out = totals
    expert_out = expert_out.astype(jnp.bfloat16)
    returned = lax.all_to_all(
        expert_out.reshape(expert_total, capacity, model_width),
        ("ctx", "head"),
        split_axis=0,
        concat_axis=0,
        tiled=True,
    )
    returned = returned.reshape(expert_total * capacity, model_width)
    gathered = returned[slot_ids.reshape(-1)].reshape(own_len, top_count, model_width)
    weights_here = combine_weights.reshape(own_len, top_count)
    mixture = jnp.sum(weights_here[..., None] * gathered.astype(jnp.float32), axis=1)
    layer_out = (residual.astype(jnp.float32) + mixture).astype(jnp.bfloat16)
    return layer_out[None]


MESH = pl.DeviceIdType.MESH
PEERS = ("z1", "z2", "z3", "x", "y", "c", "cx")
LANES = 128


def flip(value, bits):
    if bits & 1:
        value = value + 1 - 2 * (value % 2)
    if bits & 2:
        value = (value + 2) % 4
    return value


def layer_kernel(
    expert_total,
    tokens,
    attn_gain,
    wq_hbm,
    wk_hbm,
    wv_hbm,
    wo_hbm,
    moe_gain,
    chosen,
    combine,
    gate_hbm,
    up_hbm,
    down_hbm,
    cos_table,
    sin_table,
    out,
    wq,
    wk,
    wv,
    wo,
    gate,
    up,
    down,
    rows,
    kv,
    attended,
    projected,
    owned,
    gathered,
    partial,
    from_core,
    from_diag,
    from_x,
    from_y,
    from_z,
    load_sem,
    send_sem,
    recv_sem,
):
    f32, bf16 = jnp.float32, jnp.bfloat16
    ctx, h, x = lax.axis_index("ctx"), lax.axis_index("head"), lax.axis_index("pair")
    z, y = ctx // 2, ctx % 2
    ox, oy, oh = 1 - x, 1 - y, 1 - h
    seqs, own, width = tokens.shape
    block = own * 2
    head_dim = 2 * wk.shape[0]
    heads = wq.shape[1] // head_dim

    def peer(name):
        pz, py, ph, px = z, y, h, x
        if name[0] == "z":
            pz = flip(z, int(name[1]))
        if "c" in name:
            ph = oh
        if "x" in name:
            px = ox
        if "y" in name:
            py = oy
        return {"ctx": pz * 2 + py, "head": ph, "pair": px}

    loads = []
    for i, (a, b) in enumerate(
        (
            (wk_hbm, wk),
            (wv_hbm, wv),
            (wq_hbm, wq),
            (wo_hbm, wo),
            (gate_hbm.at[0], gate),
            (up_hbm.at[0], up),
            (down_hbm.at[0], down),
        )
    ):
        loads.append(pltpu.make_async_copy(a, b, load_sem.at[i]))
        loads[-1].start()

    barrier = pltpu.get_barrier_semaphore()
    for name in PEERS:
        pl.semaphore_signal(barrier, inc=1, device_id=peer(name), device_id_type=MESH)

    number = {}
    sent = []

    def copy(tag, src, dst, name):
        i = number.setdefault(tag, len(number))
        return pltpu.make_async_remote_copy(
            src_ref=src,
            dst_ref=dst,
            send_sem=send_sem.at[i],
            recv_sem=recv_sem.at[i],
            device_id=peer(name),
            device_id_type=MESH,
        )

    def send(tag, src, dst, name):
        c = copy(tag, src, dst, name)
        c.start()
        sent.append(c)

    def arrive(tag, ref, name):
        copy(tag, ref, ref, name).wait_recv()

    def norm(values, gain):
        mean_square = jnp.mean(values * values, axis=-1, keepdims=True)
        return (values * lax.rsqrt(mean_square + EPSILON) * gain).astype(bf16)

    for s in range(seqs):
        rows[x, s] = norm(tokens[s].astype(f32), attn_gain[...])
    pl.semaphore_wait(barrier, len(PEERS))
    send("rows", rows.at[x], rows.at[x], "x")

    def ordered(j):
        return jnp.concatenate([rows[0, j], rows[1, j]], axis=0)

    arrive("rows", rows.at[ox], "x")
    flat = jnp.concatenate([ordered(s) for s in range(seqs)], axis=0)
    nt = (((1,), (1,)), ((), ()))
    loads[0].wait()
    loads[1].wait()
    both = jnp.concatenate([wk[...], wv[...]], axis=0)
    kv_part = lax.dot_general(flat, both, nt, preferred_element_type=f32).astype(bf16)
    for s in range(seqs):
        kv[x, z, y, s] = kv_part[s * block : (s + 1) * block]

    def plane_start(label, at, first):
        for k in (3, 2, 1):
            send(f"{label}z{k}", at(x, z, y), at(x, z, y), f"z{k}")
        send(f"{label}x0", at(x, z, y), at(x, z, y), "x")
        send(f"{label}y0", at(x, z, y), at(x, z, y), "y")
        if first is not None:
            first("o0", at(x, z, y))

    def plane_rest(label, at, first):
        for k in (1, 2, 3):
            zk = flip(z, k)
            arrive(f"{label}z{k}", at(x, zk, y), f"z{k}")
            send(f"{label}x{k}", at(x, zk, y), at(x, zk, y), "x")
            send(f"{label}y{k}", at(x, zk, y), at(x, zk, y), "y")
            if first is not None:
                first(f"o{k}", at(x, zk, y))
        for k in range(4):
            zk = flip(z, k)
            arrive(f"{label}x{k}", at(ox, zk, y), "x")
            if k < 2:
                send(f"{label}yd{k}", at(ox, zk, y), at(ox, zk, y), "y")
            if first is not None:
                first(f"x{k}", at(ox, zk, y))
            arrive(f"{label}y{k}", at(x, zk, oy), "y")
            if k >= 2:
                send(f"{label}xd{k}", at(x, zk, oy), at(x, zk, oy), "x")
            if first is not None:
                first(f"y{k}", at(x, zk, oy))

    def plane_diag(label, at, first):
        for k in range(4):
            zk = flip(z, k)
            arrive(f"{label}{'y' if k < 2 else 'x'}d{k}", at(ox, zk, oy), "y" if k < 2 else "x")
            if first is not None:
                first(f"d{k}", at(ox, zk, oy))

    def kv_at(px, pz, py):
        return kv.at[px, pz, py]

    plane_start("kv", kv_at, None)

    loads[2].wait()
    start = pl.multiple_of(ctx * block, block)
    cos_here = cos_table[pl.ds(start, block), :]
    sin_here = sin_table[pl.ds(start, block), :]
    cos_both = jnp.concatenate([cos_here] * seqs, axis=0)
    sin_both = jnp.concatenate([sin_here] * seqs, axis=0)
    half = head_dim // 2
    queries = []
    for j in range(heads):
        q = jnp.dot(flat, wq[:, j * head_dim : (j + 1) * head_dim], preferred_element_type=f32)
        queries.append((q * cos_both + pltpu.roll(q, half, 1) * sin_both).astype(bf16))

    plane_rest("kv", kv_at, None)
    plane_diag("kv", kv_at, None)

    span = cos_table.shape[0]
    lane = lax.broadcasted_iota(jnp.int32, (span, head_dim), 1)
    row_pos = start + lax.broadcasted_iota(jnp.int32, (heads * block, span), 0) % block
    allowed = lax.broadcasted_iota(jnp.int32, (heads * block, span), 1) <= row_pos
    me = h * 2 + x
    for s in range(seqs):
        low = kv[0, :, :, s].astype(f32).reshape(span, head_dim)
        high = kv[1, :, :, s].astype(f32).reshape(span, head_dim)
        keys = jnp.where(lane < half, low, pltpu.roll(high, half, 1))
        values = jnp.where(lane < half, pltpu.roll(low, half, 1), high).astype(bf16)
        keys = (keys * cos_table[...] + pltpu.roll(keys, half, 1) * sin_table[...]).astype(bf16)
        q = jnp.concatenate([queries[j][s * block : (s + 1) * block] for j in range(heads)], axis=0)
        scores = lax.dot_general(q, keys, nt, preferred_element_type=f32) * (head_dim**-0.5)
        scores = jnp.where(allowed, scores, MASKED)
        weights = jnp.exp(scores - jnp.max(scores, axis=-1, keepdims=True))
        weights = jnp.where(allowed, weights, 0.0)
        total = jnp.sum(weights, axis=-1, keepdims=True)
        mixed = jnp.dot(weights.astype(bf16), values, preferred_element_type=f32) / total
        mixed = mixed.astype(bf16)
        for j in range(heads):
            attended[me, s * block : (s + 1) * block, j * head_dim : (j + 1) * head_dim] = mixed[
                j * block : (j + 1) * block
            ]
    for name in ("cx", "x", "c"):
        send("at" + name, attended.at[me], attended.at[me], name)
    group = {"c": (oh, x), "x": (h, ox), "cx": (oh, ox)}
    part = attended.shape[2]

    loads[3].wait()

    def term(j):
        at = pl.multiple_of(j * part, part)
        return jnp.dot(attended[j], wo[pl.ds(at, part), :], preferred_element_type=f32)

    total = term(me)
    for name in ("c", "x", "cx"):
        gh, gx = group[name]
        arrive("at" + name, attended.at[gh * 2 + gx], name)
        total = total + term(gh * 2 + gx)
    total = total.astype(bf16)
    for s in range(seqs):
        for p in range(2):
            at = s * block + p * own
            projected[s, p] = total[at : at + own]
    for name in ("cx", "x", "c"):
        gh, gx = group[name]
        send("pr" + name, projected.at[gh, gx], owned.at[me], name)
    owned[me] = projected[h, x]

    spot = lax.broadcasted_iota(jnp.int32, (own, LANES), 1)
    dense = jnp.zeros((own, LANES), f32)
    for k in range(chosen.shape[2]):
        w = jnp.broadcast_to(combine[0, :, k : k + 1], (own, LANES))
        e = jnp.broadcast_to(chosen[0, :, k : k + 1], (own, LANES))
        top = w.astype(bf16).astype(f32)
        dense = dense + jnp.where(e == spot, top, 0.0)
        dense = dense + jnp.where(e + expert_total == spot, w - top, 0.0)
    gathered[h, y, x, z, :, width:] = dense.astype(bf16)

    for name in ("c", "x", "cx"):
        gh, gx = group[name]
        arrive("pr" + name, owned.at[gh * 2 + gx], name)
    attn_out = jnp.concatenate([owned[j] for j in range(4)], axis=1)
    residual = (tokens[h].astype(f32) + attn_out.astype(f32)).astype(bf16)
    gathered[h, y, x, z, :, :width] = norm(residual.astype(f32), moe_gain[...])

    def row_at(px, pz, py):
        return gathered.at[h, py, px, pz]

    def other_core(tag, ref):
        send("core" + tag, ref, ref, "c")

    def from_other(tag, px, pz, py):
        arrive("core" + tag, gathered.at[oh, py, px, pz], "c")

    plane_start("row", row_at, other_core)
    plane_rest("row", row_at, other_core)
    for k in range(4):
        zk = flip(z, k)
        from_other(f"o{k}", x, zk, y)
        from_other(f"x{k}", ox, zk, y)

    my_expert = ctx * 2 + h
    for i in (4, 5, 6):
        loads[i].wait()
    per_side = 8 * own
    tile = min(512, width)

    def run_side(side):
        tok = jnp.concatenate(
            [gathered[g, side, :, :, :, :width].reshape(per_side, width) for g in range(2)], axis=0
        )
        marks = jnp.concatenate(
            [gathered[g, side, :, :, :, width:].reshape(per_side, LANES) for g in range(2)], axis=0
        ).astype(f32)
        col = lax.broadcasted_iota(jnp.int32, (2 * per_side, LANES), 1)
        mine = (col == my_expert) | (col == my_expert + expert_total)
        weight = jnp.sum(jnp.where(mine, marks, 0.0), axis=1, keepdims=True)
        gate_part = lax.dot_general(tok, gate[...], nt, preferred_element_type=f32)
        up_part = lax.dot_general(tok, up[...], nt, preferred_element_type=f32)
        hidden = gate_part / (1.0 + jnp.exp(-gate_part)) * up_part * weight
        hidden = hidden.astype(bf16)
        for at in range(0, width, tile):
            piece = jnp.dot(hidden, down[:, at : at + tile], preferred_element_type=f32).astype(bf16)
            for g in range(2):
                partial[g, side, :, :, :, at : at + tile] = piece[
                    g * per_side : (g + 1) * per_side
                ].reshape(2, 4, own, tile)

    run_side(y)
    for q, px in (("x", ox), ("o", x)):
        send("back" + q, partial.at[oh, y, px], from_core.at[y, px], "c")
    plane_diag("row", row_at, other_core)
    for k in range(4):
        zk = flip(z, k)
        from_other(f"y{k}", x, zk, oy)
        from_other(f"d{k}", ox, zk, oy)
    run_side(oy)
    for q, px in (("d", ox), ("y", x)):
        send("back" + q, partial.at[oh, oy, px], from_core.at[oy, px], "c")

    def join(q, py, px):
        arrive("back" + q, from_core.at[py, px], "c")
        partial[h, py, px] = (
            partial[h, py, px].astype(f32) + from_core[py, px].astype(f32)
        ).astype(bf16)

    join("x", y, ox)
    join("d", oy, ox)
    for k in range(4):
        zk = flip(z, k)
        send(f"bd{k}", partial.at[h, oy, ox, zk], from_diag.at[k], "x" if k < 2 else "y")
    for k in (1, 0):
        send(f"bx{k}", partial.at[h, y, ox, flip(z, k)], from_x.at[k], "x")
    join("y", oy, x)
    for k in (3, 2):
        send(f"by{k}", partial.at[h, oy, x, flip(z, k)], from_y.at[k], "y")
    join("o", y, x)
    for k in (3, 2):
        zk = flip(z, k)
        arrive(f"bd{k}", from_diag.at[k], "y")
        partial[h, y, ox, zk] = (
            partial[h, y, ox, zk].astype(f32) + from_diag[k].astype(f32)
        ).astype(bf16)
        send(f"bx{k}", partial.at[h, y, ox, zk], from_x.at[k], "x")
    for k in (1, 0):
        zk = flip(z, k)
        arrive(f"bd{k}", from_diag.at[k], "x")
        partial[h, oy, x, zk] = (
            partial[h, oy, x, zk].astype(f32) + from_diag[k].astype(f32)
        ).astype(bf16)
        send(f"by{k}", partial.at[h, oy, x, zk], from_y.at[k], "y")
    result = None
    for k in (3, 2, 1, 0):
        zk = flip(z, k)
        arrive(f"bx{k}", from_x.at[k], "x")
        arrive(f"by{k}", from_y.at[k], "y")
        here = partial[h, y, x, zk].astype(f32) + from_x[k].astype(f32) + from_y[k].astype(f32)
        if k:
            partial[h, y, x, zk] = here.astype(bf16)
            send(f"bz{k}", partial.at[h, y, x, zk], from_z.at[k - 1], f"z{k}")
        else:
            result = here
    for k in (1, 2, 3):
        arrive(f"bz{k}", from_z.at[k - 1], f"z{k}")
        result = result + from_z[k - 1].astype(f32)
    out[0] = (residual.astype(f32) + result).astype(bf16)
    for c in sent:
        c.wait_send()


def fused(*args):
    (
        tokens,
        attn_gain,
        wq,
        wk,
        wv,
        wo,
        moe_gain,
        chosen,
        combine,
        gate,
        up,
        down,
    ) = args
    bf16 = jnp.bfloat16
    pairs, heads, ctxs = lax.axis_size("pair"), lax.axis_size("head"), lax.axis_size("ctx")
    seqs, own, width = tokens.shape
    block = own * pairs
    span = block * ctxs
    head_dim = wk.shape[0] * pairs
    part = wq.shape[1]
    frequency = ROPE_BASE ** (-2.0 * np.arange(head_dim // 2) / head_dim)
    angles = np.arange(span)[:, None] * frequency[None, :]
    cosines, sines = np.cos(angles), np.sin(angles)
    cos_table = jnp.asarray(np.concatenate([cosines, cosines], axis=1), jnp.float32)
    sin_table = jnp.asarray(np.concatenate([-sines, sines], axis=1), jnp.float32)
    vmem = pl.BlockSpec(memory_space=pltpu.VMEM)
    anywhere = pl.BlockSpec(memory_space=pl.ANY)
    hidden = gate.shape[1]
    return pl.pallas_call(
        functools.partial(layer_kernel, ctxs * heads),
        out_shape=jax.ShapeDtypeStruct((1, own, width), bf16),
        in_specs=[vmem, vmem] + [anywhere] * 4 + [vmem] * 3 + [anywhere] * 3 + [vmem] * 2,
        out_specs=vmem,
        scratch_shapes=[
            pltpu.VMEM(wq.shape, bf16),
            pltpu.VMEM(wk.shape, bf16),
            pltpu.VMEM(wv.shape, bf16),
            pltpu.VMEM(wo.shape, bf16),
            pltpu.VMEM((hidden, width), bf16),
            pltpu.VMEM((hidden, width), bf16),
            pltpu.VMEM((hidden, width), bf16),
            pltpu.VMEM((pairs, seqs, own, width), bf16),
            pltpu.VMEM((pairs, 4, 2, seqs, block, head_dim), bf16),
            pltpu.VMEM((4, seqs * block, part), bf16),
            pltpu.VMEM((seqs, pairs, own, part), bf16),
            pltpu.VMEM((4, own, part), bf16),
            pltpu.VMEM((2, 2, 2, 4, own, width + LANES), bf16),
            pltpu.VMEM((2, 2, 2, 4, own, width), bf16),
            pltpu.VMEM((2, 2, 4, own, width), bf16),
            pltpu.VMEM((4, own, width), bf16),
            pltpu.VMEM((4, own, width), bf16),
            pltpu.VMEM((4, own, width), bf16),
            pltpu.VMEM((3, own, width), bf16),
            pltpu.SemaphoreType.DMA((7,)),
            pltpu.SemaphoreType.DMA((80,)),
            pltpu.SemaphoreType.DMA((80,)),
        ],
        compiler_params=pltpu.CompilerParams(
            collective_id=0, has_side_effects=True, vmem_limit_bytes=48 * 2**20
        ),
    )(
        tokens,
        attn_gain[None],
        wq,
        wk,
        wv,
        wo,
        moe_gain[None],
        chosen,
        combine,
        gate,
        up,
        down,
        cos_table,
        sin_table,
    )


def choose(*args):
    pairs, heads, ctxs = lax.axis_size("pair"), lax.axis_size("head"), lax.axis_size("ctx")
    seqs, own, width = args[0].shape
    experts = ctxs * heads
    fits = pairs == 2 and heads == 2 and ctxs == 8 and seqs == heads
    fits = fits and 2 * experts <= LANES and args[3].shape[0] * pairs == LANES
    return fused(*args) if fits else body(*args)


def solution(mesh):
    return jax.shard_map(
        choose,
        mesh=mesh,
        in_specs=(
            P(None, ("ctx", "pair"), None),
            P(),
            P(None, ("head", "pair")),
            P(("head", "pair"), None),
            P(("head", "pair"), None),
            P(None, ("head", "pair")),
            P(),
            P("head", ("ctx", "pair"), None),
            P("head", ("ctx", "pair"), None),
            P(("ctx", "head"), "pair", None),
            P(("ctx", "head"), "pair", None),
            P(("ctx", "head"), "pair", None),
        ),
        out_specs=P("head", ("ctx", "pair"), None),
        check_vma=False,
    )
```

```python
import functools

import jax
import jax.numpy as jnp
import numpy as np
from jax import lax
from jax.experimental import pallas as pl
from jax.experimental.pallas import tpu as pltpu
from jax.sharding import PartitionSpec as P

ROPE_BASE = 1000000.0
EPSILON = 1e-06
MASKED = -1e30


def normalize(values, gain_vector):
    wide = values.astype(jnp.float32)
    mean_square = jnp.mean(wide * wide, axis=-1, keepdims=True)
    return (wide * lax.rsqrt(mean_square + EPSILON) * gain_vector).astype(jnp.bfloat16)


def rotate(values, positions):
    half_dim = values.shape[-1] // 2
    frequency = ROPE_BASE ** (-(jnp.arange(half_dim).astype(jnp.float32) * 2.0) / values.shape[-1])
    angles = positions[:, None] * frequency[None, :]
    cosine_part = jnp.cos(angles)[:, None, :]
    sine_part = jnp.sin(angles)[:, None, :]
    lower_half = values[..., :half_dim]
    upper_half = values[..., half_dim:]
    return jnp.concatenate(
        [
            lower_half * cosine_part - upper_half * sine_part,
            upper_half * cosine_part + lower_half * sine_part,
        ],
        axis=-1,
    )


def body(
    tokens_in,
    attn_gain,
    query_matrix,
    key_matrix,
    value_matrix,
    output_matrix,
    moe_gain,
    chosen_experts,
    combine_weights,
    gate_weight,
    up_weight,
    down_weight,
):
    pair_count = lax.axis_size("pair")
    head_count = lax.axis_size("head")
    ctx_count = lax.axis_size("ctx")
    seq_count, own_len, model_width = tokens_in.shape
    block_len = own_len * pair_count
    normalized_input = normalize(tokens_in, attn_gain)
    block_rows = lax.all_gather(normalized_input, "pair", axis=1, tiled=True)
    block_start = lax.axis_index("ctx") * block_len
    query_pos = block_start + jnp.arange(block_len)
    positions = query_pos.astype(jnp.float32)
    key_part = jnp.einsum("spd,hd->sph", block_rows, key_matrix, preferred_element_type=jnp.float32)
    value_part = jnp.einsum(
        "spd,hd->sph", block_rows, value_matrix, preferred_element_type=jnp.float32
    )
    key_full, value_full = (
        lax.all_gather(key_part.astype(jnp.bfloat16), "pair", axis=2, tiled=True).astype(
            key_part.dtype
        ),
        lax.all_gather(value_part.astype(jnp.bfloat16), "pair", axis=2, tiled=True).astype(
            value_part.dtype
        ),
    )
    head_dim = key_full.shape[2]
    local_heads = query_matrix.shape[1] // head_dim
    query_unrotated = jnp.einsum(
        "spd,dh->sph", block_rows, query_matrix, preferred_element_type=jnp.float32
    )
    queries = rotate(
        query_unrotated.reshape(seq_count, block_len, local_heads, head_dim), positions
    ).astype(jnp.bfloat16)
    rotated_keys = rotate(key_full.reshape(seq_count, block_len, 1, head_dim), positions)[
        :, :, 0
    ].astype(jnp.bfloat16)
    every_value_row = value_full.astype(jnp.bfloat16)
    scaling = head_dim ** (-0.5)
    last_query = block_start + block_len - 1
    start_state = (
        jnp.full((seq_count, block_len, local_heads), MASKED, jnp.float32),
        jnp.zeros((seq_count, block_len, local_heads), jnp.float32),
        jnp.zeros((seq_count, block_len, local_heads, head_dim), jnp.float32),
    )
    key_rows = lax.all_gather(rotated_keys, "ctx", axis=1, tiled=True)
    value_rows = lax.all_gather(every_value_row, "ctx", axis=1, tiled=True)
    key_span = key_rows.shape[1]

    def compute(running_state):
        row_peak, denominator, accumulated = running_state
        key_pos = jnp.arange(key_span)
        allowed = (key_pos[None, :] <= query_pos[:, None])[None, :, None, :]
        scores = (
            jnp.einsum("sphd,skd->sphk", queries, key_rows, preferred_element_type=jnp.float32)
            * scaling
        )
        scores = jnp.where(allowed, scores, MASKED)
        new_peak = jnp.maximum(row_peak, jnp.max(scores, axis=-1))
        weights = jnp.where(allowed, jnp.exp(scores - new_peak[..., None]), 0.0)
        denominator = jnp.sum(weights, axis=-1)
        accumulated = jnp.einsum(
            "sphk,skd->sphd",
            weights.astype(jnp.bfloat16),
            value_rows,
            preferred_element_type=jnp.float32,
        )
        return (new_peak, denominator, accumulated)

    row_peak, denominator, accumulated = lax.cond(
        jnp.int32(0) > last_query, lambda skipped: skipped, compute, start_state
    )
    attended = (
        (accumulated / denominator[..., None])
        .astype(jnp.bfloat16)
        .reshape(seq_count, block_len, local_heads * head_dim)
    )
    projected = jnp.einsum(
        "sph,hc->spc",
        lax.all_gather(attended, ("head", "pair"), axis=2, tiled=True),
        output_matrix,
        preferred_element_type=jnp.float32,
    )
    projected = projected.astype(jnp.bfloat16).reshape(
        seq_count * pair_count, own_len, output_matrix.shape[1]
    )
    owned_rows = lax.all_to_all(
        projected, ("head", "pair"), split_axis=0, concat_axis=2, tiled=True
    )[0]
    own_tokens = lax.dynamic_index_in_dim(tokens_in, lax.axis_index("head"), 0, keepdims=False)
    residual = (own_tokens.astype(jnp.float32) + owned_rows.astype(jnp.float32)).astype(
        jnp.bfloat16
    )
    moe_in = normalize(residual, moe_gain)
    expert_total = ctx_count * head_count
    top_count = chosen_experts.shape[-1]
    capacity = max(2, (own_len * top_count + expert_total - 1) // expert_total + 1)
    picked = chosen_experts.reshape(own_len, top_count)
    member = (picked[..., None] == jnp.arange(expert_total)[None, None, :]).astype(jnp.int32)
    flat_count = own_len * top_count
    earlier = jnp.tril(jnp.ones((flat_count, flat_count), jnp.bfloat16))
    running = (
        jnp.dot(
            earlier,
            member.reshape(flat_count, expert_total).astype(jnp.bfloat16),
            preferred_element_type=jnp.float32,
        )
        .astype(jnp.int32)
        .reshape(own_len, top_count, expert_total)
    )
    slot_rank = jnp.sum((running - 1) * member, axis=-1)
    slot_ids = picked * capacity + slot_rank
    placing = jnp.any(
        slot_ids[..., None] == jnp.arange(expert_total * capacity)[None, None, :], axis=1
    ).astype(jnp.bfloat16)
    outgoing = jnp.einsum("ts,td->sd", placing, moe_in, preferred_element_type=jnp.float32).astype(
        jnp.bfloat16
    )
    incoming = lax.all_to_all(
        outgoing.reshape(expert_total, capacity, model_width),
        ("ctx", "head"),
        split_axis=0,
        concat_axis=0,
        tiled=True,
    )
    incoming = incoming.reshape(expert_total * capacity, model_width)
    slot_rows = incoming.shape[0]
    gate_local = gate_weight[0]
    up_local = up_weight[0]
    down_local = down_weight[0]
    quarter = gate_local.shape[0]
    totals = jnp.zeros((slot_rows, model_width), jnp.float32)
    gate_rows_w = lax.all_gather(gate_local, "pair", axis=0, tiled=True)
    up_rows_w = lax.all_gather(up_local, "pair", axis=0, tiled=True)
    down_rows_w = lax.all_gather(down_local, "pair", axis=0, tiled=True)
    for part_id in range(gate_rows_w.shape[0] // quarter):
        lower_row = part_id * quarter
        gate_part = lax.dot_general(
            gate_rows_w[lower_row : lower_row + quarter],
            incoming,
            (((1,), (1,)), ((), ())),
            preferred_element_type=jnp.float32,
        )
        up_part = lax.dot_general(
            up_rows_w[lower_row : lower_row + quarter],
            incoming,
            (((1,), (1,)), ((), ())),
            preferred_element_type=jnp.float32,
        )
        hidden = (jax.nn.silu(gate_part) * up_part).astype(jnp.bfloat16)
        partial_value = lax.dot_general(
            hidden,
            down_rows_w[lower_row : lower_row + quarter],
            (((0,), (0,)), ((), ())),
            preferred_element_type=jnp.float32,
        )
        totals = totals + lax.optimization_barrier(partial_value.astype(jnp.bfloat16)).astype(
            jnp.float32
        )
    expert_out = totals
    expert_out = expert_out.astype(jnp.bfloat16)
    returned = lax.all_to_all(
        expert_out.reshape(expert_total, capacity, model_width),
        ("ctx", "head"),
        split_axis=0,
        concat_axis=0,
        tiled=True,
    )
    returned = returned.reshape(expert_total * capacity, model_width)
    gathered = returned[slot_ids.reshape(-1)].reshape(own_len, top_count, model_width)
    weights_here = combine_weights.reshape(own_len, top_count)
    mixture = jnp.sum(weights_here[..., None] * gathered.astype(jnp.float32), axis=1)
    layer_out = (residual.astype(jnp.float32) + mixture).astype(jnp.bfloat16)
    return layer_out[None]


MESH = pl.DeviceIdType.MESH
PEERS = ("z1", "z2", "z3", "x", "y", "xy", "c", "cx")
LANES = 128


def flip(value, bits):
    if bits & 1:
        value = value + 1 - 2 * (value % 2)
    if bits & 2:
        value = (value + 2) % 4
    return value


def layer_kernel(
    expert_total,
    tokens_hbm,
    attn_gain_hbm,
    wq_hbm,
    wk_hbm,
    wv_hbm,
    wo_hbm,
    moe_gain_hbm,
    chosen_hbm,
    combine_hbm,
    gate_hbm,
    up_hbm,
    down_hbm,
    cos_hbm,
    sin_hbm,
    out,
    tokens,
    attn_gain,
    moe_gain,
    chosen,
    combine,
    cos_table,
    sin_table,
    wq,
    wk,
    wv,
    wo,
    gate,
    up,
    down,
    rows,
    kv,
    attended,
    projected,
    owned,
    gathered,
    partial,
    from_core,
    from_diag,
    from_x,
    from_y,
    from_z,
    load_sem,
    send_sem,
    recv_sem,
):
    f32, bf16 = jnp.float32, jnp.bfloat16
    ctx, h, x = lax.axis_index("ctx"), lax.axis_index("head"), lax.axis_index("pair")
    z, y = ctx // 2, ctx % 2
    ox, oy, oh = 1 - x, 1 - y, 1 - h
    seqs, own, width = tokens.shape
    block = own * 2
    head_dim = 2 * wk.shape[0]
    heads = wq.shape[1] // head_dim

    def peer(name):
        pz, py, ph, px = z, y, h, x
        if name[0] == "z":
            pz = flip(z, int(name[1]))
        if "c" in name:
            ph = oh
        if "x" in name:
            px = ox
        if "y" in name:
            py = oy
        return {"ctx": pz * 2 + py, "head": ph, "pair": px}

    loads = []
    for i, (a, b) in enumerate(
        (
            (tokens_hbm, tokens),
            (attn_gain_hbm, attn_gain),
            (wk_hbm, wk),
            (wv_hbm, wv),
            (wq_hbm, wq),
            (cos_hbm, cos_table),
            (sin_hbm, sin_table),
            (wo_hbm, wo),
            (moe_gain_hbm, moe_gain),
            (chosen_hbm.at[0], chosen),
            (combine_hbm.at[0], combine),
            (gate_hbm.at[0], gate),
            (up_hbm.at[0], up),
            (down_hbm.at[0], down),
        )
    ):
        loads.append(pltpu.make_async_copy(a, b, load_sem.at[i]))
        loads[-1].start()

    barrier = pltpu.get_barrier_semaphore()
    for name in PEERS:
        pl.semaphore_signal(barrier, inc=1, device_id=peer(name), device_id_type=MESH)

    number = {}
    sent = []

    def copy(tag, src, dst, name):
        i = number.setdefault(tag, len(number))
        return pltpu.make_async_remote_copy(
            src_ref=src,
            dst_ref=dst,
            send_sem=send_sem.at[i],
            recv_sem=recv_sem.at[i],
            device_id=peer(name),
            device_id_type=MESH,
        )

    def send(tag, src, dst, name):
        c = copy(tag, src, dst, name)
        c.start()
        sent.append(c)

    def arrive(tag, ref, name):
        copy(tag, ref, ref, name).wait_recv()

    def norm(values, gain):
        mean_square = jnp.mean(values * values, axis=-1, keepdims=True)
        return (values * lax.rsqrt(mean_square + EPSILON) * gain).astype(bf16)

    loads[0].wait()
    loads[1].wait()
    for s in range(seqs):
        rows[x, s] = norm(tokens[s].astype(f32), attn_gain[...])
    pl.semaphore_wait(barrier, len(PEERS))
    send("rows", rows.at[x], rows.at[x], "x")

    def ordered(j):
        return jnp.concatenate([rows[0, j], rows[1, j]], axis=0)

    arrive("rows", rows.at[ox], "x")
    flat = jnp.concatenate([ordered(s) for s in range(seqs)], axis=0)
    nt = (((1,), (1,)), ((), ()))
    loads[2].wait()
    loads[3].wait()
    both = jnp.concatenate([wk[...], wv[...]], axis=0)
    kv_part = lax.dot_general(flat, both, nt, preferred_element_type=f32).astype(bf16)
    for s in range(seqs):
        kv[x, z, y, s] = kv_part[s * block : (s + 1) * block]

    def plane_start(label, at, first, direct):
        for k in (3, 2, 1):
            send(f"{label}z{k}", at(x, z, y), at(x, z, y), f"z{k}")
        send(f"{label}x0", at(x, z, y), at(x, z, y), "x")
        send(f"{label}y0", at(x, z, y), at(x, z, y), "y")
        if direct:
            send(f"{label}d0", at(x, z, y), at(x, z, y), "xy")
        if first is not None:
            first("o0", at(x, z, y))

    def plane_rest(label, at, first, direct):
        for k in (1, 2, 3):
            zk = flip(z, k)
            arrive(f"{label}z{k}", at(x, zk, y), f"z{k}")
            if direct:
                send(f"{label}d{k}", at(x, zk, y), at(x, zk, y), "xy")
            send(f"{label}x{k}", at(x, zk, y), at(x, zk, y), "x")
            send(f"{label}y{k}", at(x, zk, y), at(x, zk, y), "y")
            if first is not None:
                first(f"o{k}", at(x, zk, y))
        for k in range(4):
            zk = flip(z, k)
            arrive(f"{label}x{k}", at(ox, zk, y), "x")
            if k < 2 and not direct:
                send(f"{label}yd{k}", at(ox, zk, y), at(ox, zk, y), "y")
            if first is not None:
                first(f"x{k}", at(ox, zk, y))
            arrive(f"{label}y{k}", at(x, zk, oy), "y")
            if k >= 2 and not direct:
                send(f"{label}xd{k}", at(x, zk, oy), at(x, zk, oy), "x")
            if first is not None:
                first(f"y{k}", at(x, zk, oy))

    def plane_diag(label, at, first, direct):
        for k in range(4):
            zk = flip(z, k)
            if direct:
                arrive(f"{label}d{k}", at(ox, zk, oy), "xy")
            else:
                way = "y" if k < 2 else "x"
                arrive(f"{label}{way}d{k}", at(ox, zk, oy), way)
            if first is not None:
                first(f"d{k}", at(ox, zk, oy))

    def kv_at(px, pz, py):
        return kv.at[px, pz, py]

    plane_start("kv", kv_at, None, True)

    for i in (4, 5, 6):
        loads[i].wait()
    start = pl.multiple_of(ctx * block, block)
    cos_here = cos_table[pl.ds(start, block), :]
    sin_here = sin_table[pl.ds(start, block), :]
    cos_both = jnp.concatenate([cos_here] * seqs, axis=0)
    sin_both = jnp.concatenate([sin_here] * seqs, axis=0)
    half = head_dim // 2
    queries = []
    for j in range(heads):
        q = jnp.dot(flat, wq[:, j * head_dim : (j + 1) * head_dim], preferred_element_type=f32)
        queries.append((q * cos_both + pltpu.roll(q, half, 1) * sin_both).astype(bf16))

    plane_rest("kv", kv_at, None, True)
    plane_diag("kv", kv_at, None, True)

    span = cos_table.shape[0]
    lane = lax.broadcasted_iota(jnp.int32, (span, head_dim), 1)
    row_pos = start + lax.broadcasted_iota(jnp.int32, (heads * block, span), 0) % block
    allowed = lax.broadcasted_iota(jnp.int32, (heads * block, span), 1) <= row_pos
    me = h * 2 + x
    for s in range(seqs):
        low = kv[0, :, :, s].astype(f32).reshape(span, head_dim)
        high = kv[1, :, :, s].astype(f32).reshape(span, head_dim)
        keys = jnp.where(lane < half, low, pltpu.roll(high, half, 1))
        values = jnp.where(lane < half, pltpu.roll(low, half, 1), high).astype(bf16)
        keys = (keys * cos_table[...] + pltpu.roll(keys, half, 1) * sin_table[...]).astype(bf16)
        q = jnp.concatenate([queries[j][s * block : (s + 1) * block] for j in range(heads)], axis=0)
        scores = lax.dot_general(q, keys, nt, preferred_element_type=f32) * (head_dim**-0.5)
        scores = jnp.where(allowed, scores, MASKED)
        weights = jnp.exp(scores - jnp.max(scores, axis=-1, keepdims=True))
        weights = jnp.where(allowed, weights, 0.0)
        total = jnp.sum(weights, axis=-1, keepdims=True)
        mixed = jnp.dot(weights.astype(bf16), values, preferred_element_type=f32) / total
        mixed = mixed.astype(bf16)
        for j in range(heads):
            attended[me, s * block : (s + 1) * block, j * head_dim : (j + 1) * head_dim] = mixed[
                j * block : (j + 1) * block
            ]
        for name in ("cx", "x", "c"):
            ref = attended.at[me, pl.ds(s * block, block)]
            send(f"at{s}{name}", ref, ref, name)
    group = {"c": (oh, x), "x": (h, ox), "cx": (oh, ox)}
    part = attended.shape[2]

    loads[7].wait()

    def term(j):
        at = pl.multiple_of(j * part, part)
        return jnp.dot(attended[j], wo[pl.ds(at, part), :], preferred_element_type=f32)

    total = term(me)
    for name in ("c", "x", "cx"):
        gh, gx = group[name]
        for s in range(seqs):
            arrive(f"at{s}{name}", attended.at[gh * 2 + gx, pl.ds(s * block, block)], name)
        total = total + term(gh * 2 + gx)
    total = total.astype(bf16)
    for s in range(seqs):
        for p in range(2):
            at = s * block + p * own
            projected[s, p] = total[at : at + own]
    for name in ("cx", "x", "c"):
        gh, gx = group[name]
        send("pr" + name, projected.at[gh, gx], owned.at[me], name)
    owned[me] = projected[h, x]

    for i in (8, 9, 10):
        loads[i].wait()
    spot = lax.broadcasted_iota(jnp.int32, (LANES, own), 0)
    dense = jnp.zeros((LANES, own), f32)
    for k in range(chosen.shape[0]):
        w = jnp.broadcast_to(combine[k : k + 1, :], (LANES, own))
        e = jnp.broadcast_to(chosen[k : k + 1, :], (LANES, own))
        top = w.astype(bf16).astype(f32)
        dense = dense + jnp.where(e == spot, top, 0.0)
        dense = dense + jnp.where(e + expert_total == spot, w - top, 0.0)
    ones = lax.broadcasted_iota(jnp.int32, (own, own), 0) == lax.broadcasted_iota(
        jnp.int32, (own, own), 1
    )
    dense = lax.dot_general(
        jnp.where(ones, 1.0, 0.0).astype(bf16), dense.astype(bf16), nt, preferred_element_type=f32
    )
    gathered[h, y, x, z, :, width:] = dense.astype(bf16)

    for name in ("c", "x", "cx"):
        gh, gx = group[name]
        arrive("pr" + name, owned.at[gh * 2 + gx], name)
    attn_out = jnp.concatenate([owned[j] for j in range(4)], axis=1)
    residual = (tokens[h].astype(f32) + attn_out.astype(f32)).astype(bf16)
    gathered[h, y, x, z, :, :width] = norm(residual.astype(f32), moe_gain[...])

    def row_at(px, pz, py):
        return gathered.at[h, py, px, pz]

    def other_core(tag, ref):
        send("core" + tag, ref, ref, "c")

    def from_other(tag, px, pz, py):
        arrive("core" + tag, gathered.at[oh, py, px, pz], "c")

    plane_start("row", row_at, other_core, False)
    plane_rest("row", row_at, other_core, False)
    for k in range(4):
        zk = flip(z, k)
        from_other(f"o{k}", x, zk, y)
        from_other(f"x{k}", ox, zk, y)

    my_expert = ctx * 2 + h
    for i in (11, 12, 13):
        loads[i].wait()
    per_side = 8 * own
    tile = min(512, width)

    def run_side(side):
        tok = jnp.concatenate(
            [gathered[g, side, :, :, :, :width].reshape(per_side, width) for g in range(2)], axis=0
        )
        marks = jnp.concatenate(
            [gathered[g, side, :, :, :, width:].reshape(per_side, LANES) for g in range(2)], axis=0
        ).astype(f32)
        col = lax.broadcasted_iota(jnp.int32, (2 * per_side, LANES), 1)
        mine = (col == my_expert) | (col == my_expert + expert_total)
        weight = jnp.sum(jnp.where(mine, marks, 0.0), axis=1, keepdims=True)
        gate_part = lax.dot_general(tok, gate[...], nt, preferred_element_type=f32)
        up_part = lax.dot_general(tok, up[...], nt, preferred_element_type=f32)
        hidden = gate_part / (1.0 + jnp.exp(-gate_part)) * up_part * weight
        hidden = hidden.astype(bf16)
        for at in range(0, width, tile):
            piece = jnp.dot(hidden, down[:, at : at + tile], preferred_element_type=f32).astype(bf16)
            for g in range(2):
                partial[g, side, :, :, :, at : at + tile] = piece[
                    g * per_side : (g + 1) * per_side
                ].reshape(2, 4, own, tile)

    run_side(y)
    for q, px in (("x", ox), ("o", x)):
        send("back" + q, partial.at[oh, y, px], from_core.at[y, px], "c")
    plane_diag("row", row_at, other_core, False)
    for k in range(4):
        zk = flip(z, k)
        from_other(f"y{k}", x, zk, oy)
        from_other(f"d{k}", ox, zk, oy)
    run_side(oy)
    for q, px in (("d", ox), ("y", x)):
        send("back" + q, partial.at[oh, oy, px], from_core.at[oy, px], "c")

    def join(q, py, px):
        arrive("back" + q, from_core.at[py, px], "c")
        partial[h, py, px] = (
            partial[h, py, px].astype(f32) + from_core[py, px].astype(f32)
        ).astype(bf16)

    join("x", y, ox)
    join("d", oy, ox)
    for k in range(4):
        zk = flip(z, k)
        send(f"bd{k}", partial.at[h, oy, ox, zk], from_diag.at[k], "x" if k < 2 else "y")
    for k in (1, 0):
        send(f"bx{k}", partial.at[h, y, ox, flip(z, k)], from_x.at[k], "x")
    join("y", oy, x)
    for k in (3, 2):
        send(f"by{k}", partial.at[h, oy, x, flip(z, k)], from_y.at[k], "y")
    join("o", y, x)
    for k in (3, 2):
        zk = flip(z, k)
        arrive(f"bd{k}", from_diag.at[k], "y")
        partial[h, y, ox, zk] = (
            partial[h, y, ox, zk].astype(f32) + from_diag[k].astype(f32)
        ).astype(bf16)
        send(f"bx{k}", partial.at[h, y, ox, zk], from_x.at[k], "x")
    for k in (1, 0):
        zk = flip(z, k)
        arrive(f"bd{k}", from_diag.at[k], "x")
        partial[h, oy, x, zk] = (
            partial[h, oy, x, zk].astype(f32) + from_diag[k].astype(f32)
        ).astype(bf16)
        send(f"by{k}", partial.at[h, oy, x, zk], from_y.at[k], "y")
    result = None
    for k in (3, 2, 1, 0):
        zk = flip(z, k)
        arrive(f"bx{k}", from_x.at[k], "x")
        arrive(f"by{k}", from_y.at[k], "y")
        here = partial[h, y, x, zk].astype(f32) + from_x[k].astype(f32) + from_y[k].astype(f32)
        if k:
            partial[h, y, x, zk] = here.astype(bf16)
            send(f"bz{k}", partial.at[h, y, x, zk], from_z.at[k - 1], f"z{k}")
        else:
            result = here
    for k in (1, 2, 3):
        arrive(f"bz{k}", from_z.at[k - 1], f"z{k}")
        result = result + from_z[k - 1].astype(f32)
    out[0] = (residual.astype(f32) + result).astype(bf16)
    for c in sent:
        c.wait_send()


def fused(*args):
    (
        tokens,
        attn_gain,
        wq,
        wk,
        wv,
        wo,
        moe_gain,
        chosen,
        combine,
        gate,
        up,
        down,
    ) = args
    bf16 = jnp.bfloat16
    pairs, heads, ctxs = lax.axis_size("pair"), lax.axis_size("head"), lax.axis_size("ctx")
    seqs, own, width = tokens.shape
    block = own * pairs
    span = block * ctxs
    head_dim = wk.shape[0] * pairs
    part = wq.shape[1]
    frequency = ROPE_BASE ** (-2.0 * np.arange(head_dim // 2) / head_dim)
    angles = np.arange(span)[:, None] * frequency[None, :]
    cosines, sines = np.cos(angles), np.sin(angles)
    cos_table = jnp.asarray(np.concatenate([cosines, cosines], axis=1), jnp.float32)
    sin_table = jnp.asarray(np.concatenate([-sines, sines], axis=1), jnp.float32)
    vmem = pl.BlockSpec(memory_space=pltpu.VMEM)
    anywhere = pl.BlockSpec(memory_space=pltpu.HBM)
    hidden = gate.shape[1]
    return pl.pallas_call(
        functools.partial(layer_kernel, ctxs * heads),
        out_shape=jax.ShapeDtypeStruct((1, own, width), bf16),
        in_specs=[anywhere] * 14,
        out_specs=vmem,
        scratch_shapes=[
            pltpu.VMEM(tokens.shape, bf16),
            pltpu.VMEM((1, width), jnp.float32),
            pltpu.VMEM((1, width), jnp.float32),
            pltpu.VMEM((chosen.shape[2], own), chosen.dtype),
            pltpu.VMEM((chosen.shape[2], own), jnp.float32),
            pltpu.VMEM((span, head_dim), jnp.float32),
            pltpu.VMEM((span, head_dim), jnp.float32),
            pltpu.VMEM(wq.shape, bf16),
            pltpu.VMEM(wk.shape, bf16),
            pltpu.VMEM(wv.shape, bf16),
            pltpu.VMEM(wo.shape, bf16),
            pltpu.VMEM((hidden, width), bf16),
            pltpu.VMEM((hidden, width), bf16),
            pltpu.VMEM((hidden, width), bf16),
            pltpu.VMEM((pairs, seqs, own, width), bf16),
            pltpu.VMEM((pairs, 4, 2, seqs, block, head_dim), bf16),
            pltpu.VMEM((4, seqs * block, part), bf16),
            pltpu.VMEM((seqs, pairs, own, part), bf16),
            pltpu.VMEM((4, own, part), bf16),
            pltpu.VMEM((2, 2, 2, 4, own, width + LANES), bf16),
            pltpu.VMEM((2, 2, 2, 4, own, width), bf16),
            pltpu.VMEM((2, 2, 4, own, width), bf16),
            pltpu.VMEM((4, own, width), bf16),
            pltpu.VMEM((4, own, width), bf16),
            pltpu.VMEM((4, own, width), bf16),
            pltpu.VMEM((3, own, width), bf16),
            pltpu.SemaphoreType.DMA((14,)),
            pltpu.SemaphoreType.DMA((80,)),
            pltpu.SemaphoreType.DMA((80,)),
        ],
        compiler_params=pltpu.CompilerParams(
            collective_id=0, has_side_effects=True, vmem_limit_bytes=60 * 2**20
        ),
    )(
        tokens,
        attn_gain[None],
        wq,
        wk,
        wv,
        wo,
        moe_gain[None],
        jnp.swapaxes(chosen, 1, 2),
        jnp.swapaxes(combine, 1, 2),
        gate,
        up,
        down,
        cos_table,
        sin_table,
    )


def choose(*args):
    pairs, heads, ctxs = lax.axis_size("pair"), lax.axis_size("head"), lax.axis_size("ctx")
    seqs, own, width = args[0].shape
    experts = ctxs * heads
    fits = pairs == 2 and heads == 2 and ctxs == 8 and seqs == heads
    fits = fits and 2 * experts <= LANES and args[3].shape[0] * pairs == LANES
    return fused(*args) if fits else body(*args)


def solution(mesh):
    return jax.shard_map(
        choose,
        mesh=mesh,
        in_specs=(
            P(None, ("ctx", "pair"), None),
            P(),
            P(None, ("head", "pair")),
            P(("head", "pair"), None),
            P(("head", "pair"), None),
            P(None, ("head", "pair")),
            P(),
            P("head", ("ctx", "pair"), None),
            P("head", ("ctx", "pair"), None),
            P(("ctx", "head"), "pair", None),
            P(("ctx", "head"), "pair", None),
            P(("ctx", "head"), "pair", None),
        ),
        out_specs=P("head", ("ctx", "pair"), None),
        check_vma=False,
    )
```

```python
import functools

import jax
import jax.numpy as jnp
import numpy as np
from jax import lax
from jax.experimental import pallas as pl
from jax.experimental.pallas import tpu as pltpu
from jax.sharding import PartitionSpec as P

ROPE_BASE = 1000000.0
EPSILON = 1e-06
MASKED = -1e30


def normalize(values, gain_vector):
    wide = values.astype(jnp.float32)
    mean_square = jnp.mean(wide * wide, axis=-1, keepdims=True)
    return (wide * lax.rsqrt(mean_square + EPSILON) * gain_vector).astype(jnp.bfloat16)


def rotate(values, positions):
    half_dim = values.shape[-1] // 2
    frequency = ROPE_BASE ** (-(jnp.arange(half_dim).astype(jnp.float32) * 2.0) / values.shape[-1])
    angles = positions[:, None] * frequency[None, :]
    cosine_part = jnp.cos(angles)[:, None, :]
    sine_part = jnp.sin(angles)[:, None, :]
    lower_half = values[..., :half_dim]
    upper_half = values[..., half_dim:]
    return jnp.concatenate(
        [
            lower_half * cosine_part - upper_half * sine_part,
            upper_half * cosine_part + lower_half * sine_part,
        ],
        axis=-1,
    )


def body(
    tokens_in,
    attn_gain,
    query_matrix,
    key_matrix,
    value_matrix,
    output_matrix,
    moe_gain,
    chosen_experts,
    combine_weights,
    gate_weight,
    up_weight,
    down_weight,
):
    pair_count = lax.axis_size("pair")
    head_count = lax.axis_size("head")
    ctx_count = lax.axis_size("ctx")
    seq_count, own_len, model_width = tokens_in.shape
    block_len = own_len * pair_count
    normalized_input = normalize(tokens_in, attn_gain)
    block_rows = lax.all_gather(normalized_input, "pair", axis=1, tiled=True)
    block_start = lax.axis_index("ctx") * block_len
    query_pos = block_start + jnp.arange(block_len)
    positions = query_pos.astype(jnp.float32)
    key_part = jnp.einsum("spd,hd->sph", block_rows, key_matrix, preferred_element_type=jnp.float32)
    value_part = jnp.einsum(
        "spd,hd->sph", block_rows, value_matrix, preferred_element_type=jnp.float32
    )
    key_full, value_full = (
        lax.all_gather(key_part.astype(jnp.bfloat16), "pair", axis=2, tiled=True).astype(
            key_part.dtype
        ),
        lax.all_gather(value_part.astype(jnp.bfloat16), "pair", axis=2, tiled=True).astype(
            value_part.dtype
        ),
    )
    head_dim = key_full.shape[2]
    local_heads = query_matrix.shape[1] // head_dim
    query_unrotated = jnp.einsum(
        "spd,dh->sph", block_rows, query_matrix, preferred_element_type=jnp.float32
    )
    queries = rotate(
        query_unrotated.reshape(seq_count, block_len, local_heads, head_dim), positions
    ).astype(jnp.bfloat16)
    rotated_keys = rotate(key_full.reshape(seq_count, block_len, 1, head_dim), positions)[
        :, :, 0
    ].astype(jnp.bfloat16)
    every_value_row = value_full.astype(jnp.bfloat16)
    scaling = head_dim ** (-0.5)
    last_query = block_start + block_len - 1
    start_state = (
        jnp.full((seq_count, block_len, local_heads), MASKED, jnp.float32),
        jnp.zeros((seq_count, block_len, local_heads), jnp.float32),
        jnp.zeros((seq_count, block_len, local_heads, head_dim), jnp.float32),
    )
    key_rows = lax.all_gather(rotated_keys, "ctx", axis=1, tiled=True)
    value_rows = lax.all_gather(every_value_row, "ctx", axis=1, tiled=True)
    key_span = key_rows.shape[1]

    def compute(running_state):
        row_peak, denominator, accumulated = running_state
        key_pos = jnp.arange(key_span)
        allowed = (key_pos[None, :] <= query_pos[:, None])[None, :, None, :]
        scores = (
            jnp.einsum("sphd,skd->sphk", queries, key_rows, preferred_element_type=jnp.float32)
            * scaling
        )
        scores = jnp.where(allowed, scores, MASKED)
        new_peak = jnp.maximum(row_peak, jnp.max(scores, axis=-1))
        weights = jnp.where(allowed, jnp.exp(scores - new_peak[..., None]), 0.0)
        denominator = jnp.sum(weights, axis=-1)
        accumulated = jnp.einsum(
            "sphk,skd->sphd",
            weights.astype(jnp.bfloat16),
            value_rows,
            preferred_element_type=jnp.float32,
        )
        return (new_peak, denominator, accumulated)

    row_peak, denominator, accumulated = lax.cond(
        jnp.int32(0) > last_query, lambda skipped: skipped, compute, start_state
    )
    attended = (
        (accumulated / denominator[..., None])
        .astype(jnp.bfloat16)
        .reshape(seq_count, block_len, local_heads * head_dim)
    )
    projected = jnp.einsum(
        "sph,hc->spc",
        lax.all_gather(attended, ("head", "pair"), axis=2, tiled=True),
        output_matrix,
        preferred_element_type=jnp.float32,
    )
    projected = projected.astype(jnp.bfloat16).reshape(
        seq_count * pair_count, own_len, output_matrix.shape[1]
    )
    owned_rows = lax.all_to_all(
        projected, ("head", "pair"), split_axis=0, concat_axis=2, tiled=True
    )[0]
    own_tokens = lax.dynamic_index_in_dim(tokens_in, lax.axis_index("head"), 0, keepdims=False)
    residual = (own_tokens.astype(jnp.float32) + owned_rows.astype(jnp.float32)).astype(
        jnp.bfloat16
    )
    moe_in = normalize(residual, moe_gain)
    expert_total = ctx_count * head_count
    top_count = chosen_experts.shape[-1]
    capacity = max(2, (own_len * top_count + expert_total - 1) // expert_total + 1)
    picked = chosen_experts.reshape(own_len, top_count)
    member = (picked[..., None] == jnp.arange(expert_total)[None, None, :]).astype(jnp.int32)
    flat_count = own_len * top_count
    earlier = jnp.tril(jnp.ones((flat_count, flat_count), jnp.bfloat16))
    running = (
        jnp.dot(
            earlier,
            member.reshape(flat_count, expert_total).astype(jnp.bfloat16),
            preferred_element_type=jnp.float32,
        )
        .astype(jnp.int32)
        .reshape(own_len, top_count, expert_total)
    )
    slot_rank = jnp.sum((running - 1) * member, axis=-1)
    slot_ids = picked * capacity + slot_rank
    placing = jnp.any(
        slot_ids[..., None] == jnp.arange(expert_total * capacity)[None, None, :], axis=1
    ).astype(jnp.bfloat16)
    outgoing = jnp.einsum("ts,td->sd", placing, moe_in, preferred_element_type=jnp.float32).astype(
        jnp.bfloat16
    )
    incoming = lax.all_to_all(
        outgoing.reshape(expert_total, capacity, model_width),
        ("ctx", "head"),
        split_axis=0,
        concat_axis=0,
        tiled=True,
    )
    incoming = incoming.reshape(expert_total * capacity, model_width)
    slot_rows = incoming.shape[0]
    gate_local = gate_weight[0]
    up_local = up_weight[0]
    down_local = down_weight[0]
    quarter = gate_local.shape[0]
    totals = jnp.zeros((slot_rows, model_width), jnp.float32)
    gate_rows_w = lax.all_gather(gate_local, "pair", axis=0, tiled=True)
    up_rows_w = lax.all_gather(up_local, "pair", axis=0, tiled=True)
    down_rows_w = lax.all_gather(down_local, "pair", axis=0, tiled=True)
    for part_id in range(gate_rows_w.shape[0] // quarter):
        lower_row = part_id * quarter
        gate_part = lax.dot_general(
            gate_rows_w[lower_row : lower_row + quarter],
            incoming,
            (((1,), (1,)), ((), ())),
            preferred_element_type=jnp.float32,
        )
        up_part = lax.dot_general(
            up_rows_w[lower_row : lower_row + quarter],
            incoming,
            (((1,), (1,)), ((), ())),
            preferred_element_type=jnp.float32,
        )
        hidden = (jax.nn.silu(gate_part) * up_part).astype(jnp.bfloat16)
        partial_value = lax.dot_general(
            hidden,
            down_rows_w[lower_row : lower_row + quarter],
            (((0,), (0,)), ((), ())),
            preferred_element_type=jnp.float32,
        )
        totals = totals + lax.optimization_barrier(partial_value.astype(jnp.bfloat16)).astype(
            jnp.float32
        )
    expert_out = totals
    expert_out = expert_out.astype(jnp.bfloat16)
    returned = lax.all_to_all(
        expert_out.reshape(expert_total, capacity, model_width),
        ("ctx", "head"),
        split_axis=0,
        concat_axis=0,
        tiled=True,
    )
    returned = returned.reshape(expert_total * capacity, model_width)
    gathered = returned[slot_ids.reshape(-1)].reshape(own_len, top_count, model_width)
    weights_here = combine_weights.reshape(own_len, top_count)
    mixture = jnp.sum(weights_here[..., None] * gathered.astype(jnp.float32), axis=1)
    layer_out = (residual.astype(jnp.float32) + mixture).astype(jnp.bfloat16)
    return layer_out[None]


MESH = pl.DeviceIdType.MESH
PEERS = ("z1", "z2", "z3", "x", "y", "xy", "c", "cx")
LANES = 128


def flip(value, bits):
    if bits & 1:
        value = value + 1 - 2 * (value % 2)
    if bits & 2:
        value = (value + 2) % 4
    return value


def layer_kernel(
    expert_total,
    tokens_hbm,
    attn_gain_hbm,
    wq_hbm,
    wk_hbm,
    wv_hbm,
    wo_hbm,
    moe_gain_hbm,
    chosen_hbm,
    combine_hbm,
    gate_hbm,
    up_hbm,
    down_hbm,
    cos_hbm,
    sin_hbm,
    out,
    tokens,
    attn_gain,
    moe_gain,
    chosen,
    combine,
    cos_table,
    sin_table,
    wq,
    wk,
    wv,
    wo,
    gate,
    up,
    down,
    rows,
    kv,
    attended,
    projected,
    owned,
    gathered,
    partial,
    from_core,
    from_diag,
    from_x,
    from_y,
    from_z,
    load_sem,
    send_sem,
    recv_sem,
):
    f32, bf16 = jnp.float32, jnp.bfloat16
    ctx, h, x = lax.axis_index("ctx"), lax.axis_index("head"), lax.axis_index("pair")
    z, y = ctx // 2, ctx % 2
    ox, oy, oh = 1 - x, 1 - y, 1 - h
    seqs, own, width = tokens.shape
    block = own * 2
    head_dim = 2 * wk.shape[0]
    heads = wq.shape[1] // head_dim

    def peer(name):
        pz, py, ph, px = z, y, h, x
        if name[0] == "z":
            pz = flip(z, int(name[1]))
        if "c" in name:
            ph = oh
        if "x" in name:
            px = ox
        if "y" in name:
            py = oy
        return {"ctx": pz * 2 + py, "head": ph, "pair": px}

    loads = []
    for i, (a, b) in enumerate(
        (
            (tokens_hbm, tokens),
            (attn_gain_hbm, attn_gain),
            (wk_hbm, wk),
            (wv_hbm, wv),
            (wq_hbm, wq),
            (cos_hbm, cos_table),
            (sin_hbm, sin_table),
            (wo_hbm, wo),
            (moe_gain_hbm, moe_gain),
            (chosen_hbm.at[0], chosen),
            (combine_hbm.at[0], combine),
            (gate_hbm.at[0], gate),
            (up_hbm.at[0], up),
            (down_hbm.at[0], down),
        )
    ):
        loads.append(pltpu.make_async_copy(a, b, load_sem.at[i]))
        loads[-1].start()

    barrier = pltpu.get_barrier_semaphore()
    for name in PEERS:
        pl.semaphore_signal(barrier, inc=1, device_id=peer(name), device_id_type=MESH)

    number = {}
    sent = []

    def copy(tag, src, dst, name):
        i = number.setdefault(tag, len(number))
        return pltpu.make_async_remote_copy(
            src_ref=src,
            dst_ref=dst,
            send_sem=send_sem.at[i],
            recv_sem=recv_sem.at[i],
            device_id=peer(name),
            device_id_type=MESH,
        )

    def send(tag, src, dst, name):
        c = copy(tag, src, dst, name)
        c.start()
        sent.append(c)

    def arrive(tag, ref, name):
        copy(tag, ref, ref, name).wait_recv()

    def norm(values, gain):
        mean_square = jnp.mean(values * values, axis=-1, keepdims=True)
        return (values * lax.rsqrt(mean_square + EPSILON) * gain).astype(bf16)

    loads[0].wait()
    loads[1].wait()
    for s in range(seqs):
        rows[x, s] = norm(tokens[s].astype(f32), attn_gain[...])
    pl.semaphore_wait(barrier, len(PEERS))
    send("rows", rows.at[x], rows.at[x], "x")

    def ordered(j):
        return jnp.concatenate([rows[0, j], rows[1, j]], axis=0)

    arrive("rows", rows.at[ox], "x")
    flat = jnp.concatenate([ordered(s) for s in range(seqs)], axis=0)
    nt = (((1,), (1,)), ((), ()))
    loads[2].wait()
    loads[3].wait()
    both = jnp.concatenate([wk[...], wv[...]], axis=0)
    kv_part = lax.dot_general(flat, both, nt, preferred_element_type=f32).astype(bf16)
    for s in range(seqs):
        kv[x, z, y, s] = kv_part[s * block : (s + 1) * block]

    def plane_start(label, at, first, direct):
        mine = at(x, z, y)
        send(f"{label}z1", mine, mine, "z1")
        send(f"{label}x0", mine, mine, "x")
        send(f"{label}y0", mine, mine, "y")
        send(f"{label}z2", mine, mine, "z2")
        send(f"{label}z3", mine, mine, "z3")
        if direct:
            send(f"{label}d0", mine, mine, "xy")
        if first is not None:
            first("o0", mine)

    def plane_rest(label, at, first, direct):
        def from_z(k):
            ref = at(x, flip(z, k), y)
            arrive(f"{label}z{k}", ref, f"z{k}")
            if direct:
                send(f"{label}d{k}", ref, ref, "xy")
            send(f"{label}x{k}", ref, ref, "x")
            send(f"{label}y{k}", ref, ref, "y")
            if first is not None:
                first(f"o{k}", ref)

        def from_side(way, k):
            ref = at(ox, flip(z, k), y) if way == "x" else at(x, flip(z, k), oy)
            arrive(f"{label}{way}{k}", ref, way)
            on = "y" if k % 2 == 0 else "x"
            if on != way and not direct:
                send(f"{label}d{k}", ref, ref, on)
            if first is not None:
                first(f"{way}{k}", ref)

        from_z(1)
        from_side("x", 0)
        from_side("y", 0)
        from_z(2)
        from_side("y", 1)
        from_side("x", 1)
        from_z(3)
        from_side("x", 2)
        from_side("y", 2)
        from_side("y", 3)
        from_side("x", 3)

    def plane_diag(label, at, first, direct):
        for k in range(4):
            ref = at(ox, flip(z, k), oy)
            arrive(f"{label}d{k}", ref, "xy" if direct else "y" if k % 2 == 0 else "x")
            if first is not None:
                first(f"d{k}", ref)

    def kv_at(px, pz, py):
        return kv.at[px, pz, py]

    plane_start("kv", kv_at, None, True)

    for i in (4, 5, 6):
        loads[i].wait()
    start = pl.multiple_of(ctx * block, block)
    cos_here = cos_table[pl.ds(start, block), :]
    sin_here = sin_table[pl.ds(start, block), :]
    cos_both = jnp.concatenate([cos_here] * seqs, axis=0)
    sin_both = jnp.concatenate([sin_here] * seqs, axis=0)
    half = head_dim // 2
    queries = []
    for j in range(heads):
        q = jnp.dot(flat, wq[:, j * head_dim : (j + 1) * head_dim], preferred_element_type=f32)
        queries.append((q * cos_both + pltpu.roll(q, half, 1) * sin_both).astype(bf16))

    plane_rest("kv", kv_at, None, True)
    plane_diag("kv", kv_at, None, True)

    span = cos_table.shape[0]
    lane = lax.broadcasted_iota(jnp.int32, (span, head_dim), 1)
    row_pos = start + lax.broadcasted_iota(jnp.int32, (heads * block, span), 0) % block
    allowed = lax.broadcasted_iota(jnp.int32, (heads * block, span), 1) <= row_pos
    me = h * 2 + x
    for s in range(seqs):
        low = kv[0, :, :, s].astype(f32).reshape(span, head_dim)
        high = kv[1, :, :, s].astype(f32).reshape(span, head_dim)
        keys = jnp.where(lane < half, low, pltpu.roll(high, half, 1))
        values = jnp.where(lane < half, pltpu.roll(low, half, 1), high).astype(bf16)
        keys = (keys * cos_table[...] + pltpu.roll(keys, half, 1) * sin_table[...]).astype(bf16)
        q = jnp.concatenate([queries[j][s * block : (s + 1) * block] for j in range(heads)], axis=0)
        scores = lax.dot_general(q, keys, nt, preferred_element_type=f32) * (head_dim**-0.5)
        scores = jnp.where(allowed, scores, MASKED)
        weights = jnp.exp(scores - jnp.max(scores, axis=-1, keepdims=True))
        weights = jnp.where(allowed, weights, 0.0)
        total = jnp.sum(weights, axis=-1, keepdims=True)
        mixed = jnp.dot(weights.astype(bf16), values, preferred_element_type=f32) / total
        mixed = mixed.astype(bf16)
        for j in range(heads):
            attended[me, s * block : (s + 1) * block, j * head_dim : (j + 1) * head_dim] = mixed[
                j * block : (j + 1) * block
            ]
        for name in ("cx", "x", "c"):
            ref = attended.at[me, pl.ds(s * block, block)]
            send(f"at{s}{name}", ref, ref, name)
    group = {"c": (oh, x), "x": (h, ox), "cx": (oh, ox)}
    part = attended.shape[2]

    loads[7].wait()

    def term(j):
        at = pl.multiple_of(j * part, part)
        return jnp.dot(attended[j], wo[pl.ds(at, part), :], preferred_element_type=f32)

    total = term(me)
    for name in ("c", "x", "cx"):
        gh, gx = group[name]
        for s in range(seqs):
            arrive(f"at{s}{name}", attended.at[gh * 2 + gx, pl.ds(s * block, block)], name)
        total = total + term(gh * 2 + gx)
    total = total.astype(bf16)
    for s in range(seqs):
        for p in range(2):
            at = s * block + p * own
            projected[s, p] = total[at : at + own]
    for name in ("cx", "x", "c"):
        gh, gx = group[name]
        send("pr" + name, projected.at[gh, gx], owned.at[me], name)
    owned[me] = projected[h, x]

    for i in (8, 9, 10):
        loads[i].wait()
    spot = lax.broadcasted_iota(jnp.int32, (LANES, own), 0)
    dense = jnp.zeros((LANES, own), f32)
    for k in range(chosen.shape[0]):
        w = jnp.broadcast_to(combine[k : k + 1, :], (LANES, own))
        e = jnp.broadcast_to(chosen[k : k + 1, :], (LANES, own))
        top = w.astype(bf16).astype(f32)
        dense = dense + jnp.where(e == spot, top, 0.0)
        dense = dense + jnp.where(e + expert_total == spot, w - top, 0.0)
    ones = lax.broadcasted_iota(jnp.int32, (own, own), 0) == lax.broadcasted_iota(
        jnp.int32, (own, own), 1
    )
    dense = lax.dot_general(
        jnp.where(ones, 1.0, 0.0).astype(bf16), dense.astype(bf16), nt, preferred_element_type=f32
    )
    gathered[h, y, x, z, :, width:] = dense.astype(bf16)

    for name in ("c", "x", "cx"):
        gh, gx = group[name]
        arrive("pr" + name, owned.at[gh * 2 + gx], name)
    attn_out = jnp.concatenate([owned[j] for j in range(4)], axis=1)
    residual = (tokens[h].astype(f32) + attn_out.astype(f32)).astype(bf16)
    gathered[h, y, x, z, :, :width] = norm(residual.astype(f32), moe_gain[...])

    def row_at(px, pz, py):
        return gathered.at[h, py, px, pz]

    def other_core(tag, ref):
        send("core" + tag, ref, ref, "c")

    def from_other(tag, px, pz, py):
        arrive("core" + tag, gathered.at[oh, py, px, pz], "c")

    plane_start("row", row_at, other_core, False)
    plane_rest("row", row_at, other_core, False)
    for k in range(4):
        zk = flip(z, k)
        from_other(f"o{k}", x, zk, y)
        from_other(f"x{k}", ox, zk, y)

    my_expert = ctx * 2 + h
    for i in (11, 12, 13):
        loads[i].wait()
    per_side = 8 * own
    tile = min(512, width)

    def run_side(side):
        tok = jnp.concatenate(
            [gathered[g, side, :, :, :, :width].reshape(per_side, width) for g in range(2)], axis=0
        )
        marks = jnp.concatenate(
            [gathered[g, side, :, :, :, width:].reshape(per_side, LANES) for g in range(2)], axis=0
        ).astype(f32)
        col = lax.broadcasted_iota(jnp.int32, (2 * per_side, LANES), 1)
        mine = (col == my_expert) | (col == my_expert + expert_total)
        weight = jnp.sum(jnp.where(mine, marks, 0.0), axis=1, keepdims=True)
        gate_part = lax.dot_general(tok, gate[...], nt, preferred_element_type=f32)
        up_part = lax.dot_general(tok, up[...], nt, preferred_element_type=f32)
        hidden = gate_part / (1.0 + jnp.exp(-gate_part)) * up_part * weight
        hidden = hidden.astype(bf16)
        for at in range(0, width, tile):
            piece = jnp.dot(hidden, down[:, at : at + tile], preferred_element_type=f32).astype(bf16)
            for g in range(2):
                partial[g, side, :, :, :, at : at + tile] = piece[
                    g * per_side : (g + 1) * per_side
                ].reshape(2, 4, own, tile)

    run_side(y)
    for q, px in (("x", ox), ("o", x)):
        send("back" + q, partial.at[oh, y, px], from_core.at[y, px], "c")
    plane_diag("row", row_at, other_core, False)
    for k in range(4):
        zk = flip(z, k)
        from_other(f"y{k}", x, zk, oy)
        from_other(f"d{k}", ox, zk, oy)
    run_side(oy)
    for q, px in (("d", ox), ("y", x)):
        send("back" + q, partial.at[oh, oy, px], from_core.at[oy, px], "c")

    def join(q, py, px):
        arrive("back" + q, from_core.at[py, px], "c")
        partial[h, py, px] = (
            partial[h, py, px].astype(f32) + from_core[py, px].astype(f32)
        ).astype(bf16)

    def diag_send(k):
        send(f"bd{k}", partial.at[h, oy, ox, flip(z, k)], from_diag.at[k], "x" if k % 2 else "y")

    def side_send(way, k, after_diag):
        py, px = (y, ox) if way == "x" else (oy, x)
        zk = flip(z, k)
        if after_diag:
            arrive(f"bd{k}", from_diag.at[k], "x" if k % 2 else "y")
            partial[h, py, px, zk] = (
                partial[h, py, px, zk].astype(f32) + from_diag[k].astype(f32)
            ).astype(bf16)
        there = from_x if way == "x" else from_y
        send(f"b{way}{k}", partial.at[h, py, px, zk], there.at[k], way)

    join("d", oy, ox)
    diag_send(3)
    diag_send(2)
    join("x", y, ox)
    side_send("x", 3, False)
    join("y", oy, x)
    side_send("y", 2, False)
    side_send("y", 3, True)
    side_send("x", 2, True)
    diag_send(1)
    diag_send(0)
    side_send("x", 1, False)
    join("o", y, x)
    side_send("y", 1, True)
    side_send("y", 0, False)
    side_send("x", 0, True)
    result = None
    for k in (3, 2, 1, 0):
        zk = flip(z, k)
        arrive(f"bx{k}", from_x.at[k], "x")
        arrive(f"by{k}", from_y.at[k], "y")
        here = partial[h, y, x, zk].astype(f32) + from_x[k].astype(f32) + from_y[k].astype(f32)
        if k:
            partial[h, y, x, zk] = here.astype(bf16)
            send(f"bz{k}", partial.at[h, y, x, zk], from_z.at[k - 1], f"z{k}")
        else:
            result = here
    for k in (1, 2, 3):
        arrive(f"bz{k}", from_z.at[k - 1], f"z{k}")
        result = result + from_z[k - 1].astype(f32)
    out[0] = (residual.astype(f32) + result).astype(bf16)
    for c in sent:
        c.wait_send()


def fused(*args):
    (
        tokens,
        attn_gain,
        wq,
        wk,
        wv,
        wo,
        moe_gain,
        chosen,
        combine,
        gate,
        up,
        down,
    ) = args
    bf16 = jnp.bfloat16
    pairs, heads, ctxs = lax.axis_size("pair"), lax.axis_size("head"), lax.axis_size("ctx")
    seqs, own, width = tokens.shape
    block = own * pairs
    span = block * ctxs
    head_dim = wk.shape[0] * pairs
    part = wq.shape[1]
    frequency = ROPE_BASE ** (-2.0 * np.arange(head_dim // 2) / head_dim)
    angles = np.arange(span)[:, None] * frequency[None, :]
    cosines, sines = np.cos(angles), np.sin(angles)
    cos_table = jnp.asarray(np.concatenate([cosines, cosines], axis=1), jnp.float32)
    sin_table = jnp.asarray(np.concatenate([-sines, sines], axis=1), jnp.float32)
    vmem = pl.BlockSpec(memory_space=pltpu.VMEM)
    anywhere = pl.BlockSpec(memory_space=pltpu.HBM)
    hidden = gate.shape[1]
    return pl.pallas_call(
        functools.partial(layer_kernel, ctxs * heads),
        out_shape=jax.ShapeDtypeStruct((1, own, width), bf16),
        in_specs=[anywhere] * 14,
        out_specs=vmem,
        scratch_shapes=[
            pltpu.VMEM(tokens.shape, bf16),
            pltpu.VMEM((1, width), jnp.float32),
            pltpu.VMEM((1, width), jnp.float32),
            pltpu.VMEM((chosen.shape[2], own), chosen.dtype),
            pltpu.VMEM((chosen.shape[2], own), jnp.float32),
            pltpu.VMEM((span, head_dim), jnp.float32),
            pltpu.VMEM((span, head_dim), jnp.float32),
            pltpu.VMEM(wq.shape, bf16),
            pltpu.VMEM(wk.shape, bf16),
            pltpu.VMEM(wv.shape, bf16),
            pltpu.VMEM(wo.shape, bf16),
            pltpu.VMEM((hidden, width), bf16),
            pltpu.VMEM((hidden, width), bf16),
            pltpu.VMEM((hidden, width), bf16),
            pltpu.VMEM((pairs, seqs, own, width), bf16),
            pltpu.VMEM((pairs, 4, 2, seqs, block, head_dim), bf16),
            pltpu.VMEM((4, seqs * block, part), bf16),
            pltpu.VMEM((seqs, pairs, own, part), bf16),
            pltpu.VMEM((4, own, part), bf16),
            pltpu.VMEM((2, 2, 2, 4, own, width + LANES), bf16),
            pltpu.VMEM((2, 2, 2, 4, own, width), bf16),
            pltpu.VMEM((2, 2, 4, own, width), bf16),
            pltpu.VMEM((4, own, width), bf16),
            pltpu.VMEM((4, own, width), bf16),
            pltpu.VMEM((4, own, width), bf16),
            pltpu.VMEM((3, own, width), bf16),
            pltpu.SemaphoreType.DMA((14,)),
            pltpu.SemaphoreType.DMA((80,)),
            pltpu.SemaphoreType.DMA((80,)),
        ],
        compiler_params=pltpu.CompilerParams(
            collective_id=0, has_side_effects=True, vmem_limit_bytes=60 * 2**20
        ),
    )(
        tokens,
        attn_gain[None],
        wq,
        wk,
        wv,
        wo,
        moe_gain[None],
        jnp.swapaxes(chosen, 1, 2),
        jnp.swapaxes(combine, 1, 2),
        gate,
        up,
        down,
        cos_table,
        sin_table,
    )


def choose(*args):
    pairs, heads, ctxs = lax.axis_size("pair"), lax.axis_size("head"), lax.axis_size("ctx")
    seqs, own, width = args[0].shape
    experts = ctxs * heads
    fits = pairs == 2 and heads == 2 and ctxs == 8 and seqs == heads
    fits = fits and 2 * experts <= LANES and args[3].shape[0] * pairs == LANES
    return fused(*args) if fits else body(*args)


def solution(mesh):
    return jax.shard_map(
        choose,
        mesh=mesh,
        in_specs=(
            P(None, ("ctx", "pair"), None),
            P(),
            P(None, ("head", "pair")),
            P(("head", "pair"), None),
            P(("head", "pair"), None),
            P(None, ("head", "pair")),
            P(),
            P("head", ("ctx", "pair"), None),
            P("head", ("ctx", "pair"), None),
            P(("ctx", "head"), "pair", None),
            P(("ctx", "head"), "pair", None),
            P(("ctx", "head"), "pair", None),
        ),
        out_specs=P("head", ("ctx", "pair"), None),
        check_vma=False,
    )
```

```python
import functools

import jax
import jax.numpy as jnp
import numpy as np
from jax import lax
from jax.experimental import pallas as pl
from jax.experimental.pallas import tpu as pltpu
from jax.sharding import PartitionSpec as P

ROPE_BASE = 1000000.0
EPSILON = 1e-06
MASKED = -1e30


def normalize(values, gain_vector):
    wide = values.astype(jnp.float32)
    mean_square = jnp.mean(wide * wide, axis=-1, keepdims=True)
    return (wide * lax.rsqrt(mean_square + EPSILON) * gain_vector).astype(jnp.bfloat16)


def rotate(values, positions):
    half_dim = values.shape[-1] // 2
    frequency = ROPE_BASE ** (-(jnp.arange(half_dim).astype(jnp.float32) * 2.0) / values.shape[-1])
    angles = positions[:, None] * frequency[None, :]
    cosine_part = jnp.cos(angles)[:, None, :]
    sine_part = jnp.sin(angles)[:, None, :]
    lower_half = values[..., :half_dim]
    upper_half = values[..., half_dim:]
    return jnp.concatenate(
        [
            lower_half * cosine_part - upper_half * sine_part,
            upper_half * cosine_part + lower_half * sine_part,
        ],
        axis=-1,
    )


def body(
    tokens_in,
    attn_gain,
    query_matrix,
    key_matrix,
    value_matrix,
    output_matrix,
    moe_gain,
    chosen_experts,
    combine_weights,
    gate_weight,
    up_weight,
    down_weight,
):
    pair_count = lax.axis_size("pair")
    head_count = lax.axis_size("head")
    ctx_count = lax.axis_size("ctx")
    seq_count, own_len, model_width = tokens_in.shape
    block_len = own_len * pair_count
    normalized_input = normalize(tokens_in, attn_gain)
    block_rows = lax.all_gather(normalized_input, "pair", axis=1, tiled=True)
    block_start = lax.axis_index("ctx") * block_len
    query_pos = block_start + jnp.arange(block_len)
    positions = query_pos.astype(jnp.float32)
    key_part = jnp.einsum("spd,hd->sph", block_rows, key_matrix, preferred_element_type=jnp.float32)
    value_part = jnp.einsum(
        "spd,hd->sph", block_rows, value_matrix, preferred_element_type=jnp.float32
    )
    key_full, value_full = (
        lax.all_gather(key_part.astype(jnp.bfloat16), "pair", axis=2, tiled=True).astype(
            key_part.dtype
        ),
        lax.all_gather(value_part.astype(jnp.bfloat16), "pair", axis=2, tiled=True).astype(
            value_part.dtype
        ),
    )
    head_dim = key_full.shape[2]
    local_heads = query_matrix.shape[1] // head_dim
    query_unrotated = jnp.einsum(
        "spd,dh->sph", block_rows, query_matrix, preferred_element_type=jnp.float32
    )
    queries = rotate(
        query_unrotated.reshape(seq_count, block_len, local_heads, head_dim), positions
    ).astype(jnp.bfloat16)
    rotated_keys = rotate(key_full.reshape(seq_count, block_len, 1, head_dim), positions)[
        :, :, 0
    ].astype(jnp.bfloat16)
    every_value_row = value_full.astype(jnp.bfloat16)
    scaling = head_dim ** (-0.5)
    last_query = block_start + block_len - 1
    start_state = (
        jnp.full((seq_count, block_len, local_heads), MASKED, jnp.float32),
        jnp.zeros((seq_count, block_len, local_heads), jnp.float32),
        jnp.zeros((seq_count, block_len, local_heads, head_dim), jnp.float32),
    )
    key_rows = lax.all_gather(rotated_keys, "ctx", axis=1, tiled=True)
    value_rows = lax.all_gather(every_value_row, "ctx", axis=1, tiled=True)
    key_span = key_rows.shape[1]

    def compute(running_state):
        row_peak, denominator, accumulated = running_state
        key_pos = jnp.arange(key_span)
        allowed = (key_pos[None, :] <= query_pos[:, None])[None, :, None, :]
        scores = (
            jnp.einsum("sphd,skd->sphk", queries, key_rows, preferred_element_type=jnp.float32)
            * scaling
        )
        scores = jnp.where(allowed, scores, MASKED)
        new_peak = jnp.maximum(row_peak, jnp.max(scores, axis=-1))
        weights = jnp.where(allowed, jnp.exp(scores - new_peak[..., None]), 0.0)
        denominator = jnp.sum(weights, axis=-1)
        accumulated = jnp.einsum(
            "sphk,skd->sphd",
            weights.astype(jnp.bfloat16),
            value_rows,
            preferred_element_type=jnp.float32,
        )
        return (new_peak, denominator, accumulated)

    row_peak, denominator, accumulated = lax.cond(
        jnp.int32(0) > last_query, lambda skipped: skipped, compute, start_state
    )
    attended = (
        (accumulated / denominator[..., None])
        .astype(jnp.bfloat16)
        .reshape(seq_count, block_len, local_heads * head_dim)
    )
    projected = jnp.einsum(
        "sph,hc->spc",
        lax.all_gather(attended, ("head", "pair"), axis=2, tiled=True),
        output_matrix,
        preferred_element_type=jnp.float32,
    )
    projected = projected.astype(jnp.bfloat16).reshape(
        seq_count * pair_count, own_len, output_matrix.shape[1]
    )
    owned_rows = lax.all_to_all(
        projected, ("head", "pair"), split_axis=0, concat_axis=2, tiled=True
    )[0]
    own_tokens = lax.dynamic_index_in_dim(tokens_in, lax.axis_index("head"), 0, keepdims=False)
    residual = (own_tokens.astype(jnp.float32) + owned_rows.astype(jnp.float32)).astype(
        jnp.bfloat16
    )
    moe_in = normalize(residual, moe_gain)
    expert_total = ctx_count * head_count
    top_count = chosen_experts.shape[-1]
    capacity = max(2, (own_len * top_count + expert_total - 1) // expert_total + 1)
    picked = chosen_experts.reshape(own_len, top_count)
    member = (picked[..., None] == jnp.arange(expert_total)[None, None, :]).astype(jnp.int32)
    flat_count = own_len * top_count
    earlier = jnp.tril(jnp.ones((flat_count, flat_count), jnp.bfloat16))
    running = (
        jnp.dot(
            earlier,
            member.reshape(flat_count, expert_total).astype(jnp.bfloat16),
            preferred_element_type=jnp.float32,
        )
        .astype(jnp.int32)
        .reshape(own_len, top_count, expert_total)
    )
    slot_rank = jnp.sum((running - 1) * member, axis=-1)
    slot_ids = picked * capacity + slot_rank
    placing = jnp.any(
        slot_ids[..., None] == jnp.arange(expert_total * capacity)[None, None, :], axis=1
    ).astype(jnp.bfloat16)
    outgoing = jnp.einsum("ts,td->sd", placing, moe_in, preferred_element_type=jnp.float32).astype(
        jnp.bfloat16
    )
    incoming = lax.all_to_all(
        outgoing.reshape(expert_total, capacity, model_width),
        ("ctx", "head"),
        split_axis=0,
        concat_axis=0,
        tiled=True,
    )
    incoming = incoming.reshape(expert_total * capacity, model_width)
    slot_rows = incoming.shape[0]
    gate_local = gate_weight[0]
    up_local = up_weight[0]
    down_local = down_weight[0]
    quarter = gate_local.shape[0]
    totals = jnp.zeros((slot_rows, model_width), jnp.float32)
    gate_rows_w = lax.all_gather(gate_local, "pair", axis=0, tiled=True)
    up_rows_w = lax.all_gather(up_local, "pair", axis=0, tiled=True)
    down_rows_w = lax.all_gather(down_local, "pair", axis=0, tiled=True)
    for part_id in range(gate_rows_w.shape[0] // quarter):
        lower_row = part_id * quarter
        gate_part = lax.dot_general(
            gate_rows_w[lower_row : lower_row + quarter],
            incoming,
            (((1,), (1,)), ((), ())),
            preferred_element_type=jnp.float32,
        )
        up_part = lax.dot_general(
            up_rows_w[lower_row : lower_row + quarter],
            incoming,
            (((1,), (1,)), ((), ())),
            preferred_element_type=jnp.float32,
        )
        hidden = (jax.nn.silu(gate_part) * up_part).astype(jnp.bfloat16)
        partial_value = lax.dot_general(
            hidden,
            down_rows_w[lower_row : lower_row + quarter],
            (((0,), (0,)), ((), ())),
            preferred_element_type=jnp.float32,
        )
        totals = totals + lax.optimization_barrier(partial_value.astype(jnp.bfloat16)).astype(
            jnp.float32
        )
    expert_out = totals
    expert_out = expert_out.astype(jnp.bfloat16)
    returned = lax.all_to_all(
        expert_out.reshape(expert_total, capacity, model_width),
        ("ctx", "head"),
        split_axis=0,
        concat_axis=0,
        tiled=True,
    )
    returned = returned.reshape(expert_total * capacity, model_width)
    gathered = returned[slot_ids.reshape(-1)].reshape(own_len, top_count, model_width)
    weights_here = combine_weights.reshape(own_len, top_count)
    mixture = jnp.sum(weights_here[..., None] * gathered.astype(jnp.float32), axis=1)
    layer_out = (residual.astype(jnp.float32) + mixture).astype(jnp.bfloat16)
    return layer_out[None]


MESH = pl.DeviceIdType.MESH
PEERS = ("z1", "z2", "z3", "x", "y", "xy", "c", "cx")
LANES = 128


def flip(value, bits):
    if bits & 1:
        value = value + 1 - 2 * (value % 2)
    if bits & 2:
        value = (value + 2) % 4
    return value


def layer_kernel(
    expert_total,
    tokens_hbm,
    attn_gain_hbm,
    wq_hbm,
    wk_hbm,
    wv_hbm,
    wo_hbm,
    moe_gain_hbm,
    chosen_hbm,
    combine_hbm,
    gate_hbm,
    up_hbm,
    down_hbm,
    cos_hbm,
    sin_hbm,
    out,
    tokens,
    attn_gain,
    moe_gain,
    chosen,
    combine,
    cos_table,
    sin_table,
    wq,
    wk,
    wv,
    wo,
    gate,
    up,
    down,
    rows,
    kv,
    attended,
    projected,
    owned,
    gathered,
    partial,
    from_core,
    from_diag,
    from_x,
    from_y,
    from_z,
    load_sem,
    send_sem,
    recv_sem,
):
    f32, bf16 = jnp.float32, jnp.bfloat16
    ctx, h, x = lax.axis_index("ctx"), lax.axis_index("head"), lax.axis_index("pair")
    z, y = ctx // 2, ctx % 2
    ox, oy, oh = 1 - x, 1 - y, 1 - h
    seqs, own, width = tokens.shape
    block = own * 2
    head_dim = 2 * wk.shape[0]
    heads = wq.shape[1] // head_dim

    def peer(name):
        pz, py, ph, px = z, y, h, x
        if name[0] == "z":
            pz = flip(z, int(name[1]))
        if "c" in name:
            ph = oh
        if "x" in name:
            px = ox
        if "y" in name:
            py = oy
        return {"ctx": pz * 2 + py, "head": ph, "pair": px}

    loads = []
    for i, (a, b) in enumerate(
        (
            (tokens_hbm, tokens),
            (attn_gain_hbm, attn_gain),
            (wk_hbm, wk),
            (wv_hbm, wv),
            (wq_hbm, wq),
            (cos_hbm, cos_table),
            (sin_hbm, sin_table),
            (wo_hbm, wo),
            (moe_gain_hbm, moe_gain),
            (chosen_hbm.at[0], chosen),
            (combine_hbm.at[0], combine),
            (gate_hbm.at[0], gate),
            (up_hbm.at[0], up),
            (down_hbm.at[0], down),
        )
    ):
        loads.append(pltpu.make_async_copy(a, b, load_sem.at[i]))
        loads[-1].start()

    barrier = pltpu.get_barrier_semaphore()
    for name in PEERS:
        pl.semaphore_signal(barrier, inc=1, device_id=peer(name), device_id_type=MESH)

    number = {}
    sent = []

    def copy(tag, src, dst, name):
        i = number.setdefault(tag, len(number))
        return pltpu.make_async_remote_copy(
            src_ref=src,
            dst_ref=dst,
            send_sem=send_sem.at[i],
            recv_sem=recv_sem.at[i],
            device_id=peer(name),
            device_id_type=MESH,
        )

    def send(tag, src, dst, name):
        c = copy(tag, src, dst, name)
        c.start()
        sent.append(c)

    def arrive(tag, ref, name):
        copy(tag, ref, ref, name).wait_recv()

    def norm(values, gain):
        mean_square = jnp.mean(values * values, axis=-1, keepdims=True)
        return (values * lax.rsqrt(mean_square + EPSILON) * gain).astype(bf16)

    loads[0].wait()
    loads[1].wait()
    for s in range(seqs):
        rows[x, s] = norm(tokens[s].astype(f32), attn_gain[...])
    pl.semaphore_wait(barrier, len(PEERS))
    send("rows", rows.at[x], rows.at[x], "x")

    def ordered(j):
        return jnp.concatenate([rows[0, j], rows[1, j]], axis=0)

    arrive("rows", rows.at[ox], "x")
    flat = jnp.concatenate([ordered(s) for s in range(seqs)], axis=0)
    nt = (((1,), (1,)), ((), ()))
    loads[2].wait()
    loads[3].wait()
    both = jnp.concatenate([wk[...], wv[...]], axis=0)
    kv_part = lax.dot_general(flat, both, nt, preferred_element_type=f32).astype(bf16)
    for s in range(seqs):
        kv[x, z, y, s] = kv_part[s * block : (s + 1) * block]

    def plane_start(label, at, first, direct):
        for k in (3, 2, 1):
            send(f"{label}z{k}", at(x, z, y), at(x, z, y), f"z{k}")
        send(f"{label}x0", at(x, z, y), at(x, z, y), "x")
        send(f"{label}y0", at(x, z, y), at(x, z, y), "y")
        if direct:
            send(f"{label}d0", at(x, z, y), at(x, z, y), "xy")
        if first is not None:
            first("o0", at(x, z, y))

    def plane_rest(label, at, first, direct):
        for k in (1, 2, 3):
            zk = flip(z, k)
            arrive(f"{label}z{k}", at(x, zk, y), f"z{k}")
            if direct:
                send(f"{label}d{k}", at(x, zk, y), at(x, zk, y), "xy")
            send(f"{label}x{k}", at(x, zk, y), at(x, zk, y), "x")
            send(f"{label}y{k}", at(x, zk, y), at(x, zk, y), "y")
            if first is not None:
                first(f"o{k}", at(x, zk, y))
        for k in range(4):
            zk = flip(z, k)
            arrive(f"{label}x{k}", at(ox, zk, y), "x")
            if k < 2 and not direct:
                send(f"{label}yd{k}", at(ox, zk, y), at(ox, zk, y), "y")
            if first is not None:
                first(f"x{k}", at(ox, zk, y))
            arrive(f"{label}y{k}", at(x, zk, oy), "y")
            if k >= 2 and not direct:
                send(f"{label}xd{k}", at(x, zk, oy), at(x, zk, oy), "x")
            if first is not None:
                first(f"y{k}", at(x, zk, oy))

    def plane_diag(label, at, first, direct):
        for k in range(4):
            zk = flip(z, k)
            if direct:
                arrive(f"{label}d{k}", at(ox, zk, oy), "xy")
            else:
                way = "y" if k < 2 else "x"
                arrive(f"{label}{way}d{k}", at(ox, zk, oy), way)
            if first is not None:
                first(f"d{k}", at(ox, zk, oy))

    def kv_at(px, pz, py):
        return kv.at[px, pz, py]

    plane_start("kv", kv_at, None, True)

    for i in (4, 5, 6):
        loads[i].wait()
    start = pl.multiple_of(ctx * block, block)
    cos_here = cos_table[pl.ds(start, block), :]
    sin_here = sin_table[pl.ds(start, block), :]
    cos_both = jnp.concatenate([cos_here] * seqs, axis=0)
    sin_both = jnp.concatenate([sin_here] * seqs, axis=0)
    half = head_dim // 2
    queries = []
    for j in range(heads):
        q = jnp.dot(flat, wq[:, j * head_dim : (j + 1) * head_dim], preferred_element_type=f32)
        queries.append((q * cos_both + pltpu.roll(q, half, 1) * sin_both).astype(bf16))

    plane_rest("kv", kv_at, None, True)
    plane_diag("kv", kv_at, None, True)

    span = cos_table.shape[0]
    lane = lax.broadcasted_iota(jnp.int32, (span, head_dim), 1)
    row_pos = start + lax.broadcasted_iota(jnp.int32, (heads * block, span), 0) % block
    allowed = lax.broadcasted_iota(jnp.int32, (heads * block, span), 1) <= row_pos
    me = h * 2 + x
    for s in range(seqs):
        low = kv[0, :, :, s].astype(f32).reshape(span, head_dim)
        high = kv[1, :, :, s].astype(f32).reshape(span, head_dim)
        keys = jnp.where(lane < half, low, pltpu.roll(high, half, 1))
        values = jnp.where(lane < half, pltpu.roll(low, half, 1), high).astype(bf16)
        keys = (keys * cos_table[...] + pltpu.roll(keys, half, 1) * sin_table[...]).astype(bf16)
        q = jnp.concatenate([queries[j][s * block : (s + 1) * block] for j in range(heads)], axis=0)
        scores = lax.dot_general(q, keys, nt, preferred_element_type=f32) * (head_dim**-0.5)
        scores = jnp.where(allowed, scores, MASKED)
        weights = jnp.exp(scores - jnp.max(scores, axis=-1, keepdims=True))
        weights = jnp.where(allowed, weights, 0.0)
        total = jnp.sum(weights, axis=-1, keepdims=True)
        mixed = jnp.dot(weights.astype(bf16), values, preferred_element_type=f32) / total
        mixed = mixed.astype(bf16)
        for j in range(heads):
            attended[me, s * block : (s + 1) * block, j * head_dim : (j + 1) * head_dim] = mixed[
                j * block : (j + 1) * block
            ]
        for name in ("cx", "x", "c"):
            ref = attended.at[me, pl.ds(s * block, block)]
            send(f"at{s}{name}", ref, ref, name)
    group = {"c": (oh, x), "x": (h, ox), "cx": (oh, ox)}
    part = attended.shape[2]

    loads[7].wait()

    def term(j):
        at = pl.multiple_of(j * part, part)
        return jnp.dot(attended[j], wo[pl.ds(at, part), :], preferred_element_type=f32)

    total = term(me)
    for name in ("c", "x", "cx"):
        gh, gx = group[name]
        for s in range(seqs):
            arrive(f"at{s}{name}", attended.at[gh * 2 + gx, pl.ds(s * block, block)], name)
        total = total + term(gh * 2 + gx)
    total = total.astype(bf16)
    for s in range(seqs):
        for p in range(2):
            at = s * block + p * own
            projected[s, p] = total[at : at + own]
    for name in ("cx", "x", "c"):
        gh, gx = group[name]
        send("pr" + name, projected.at[gh, gx], owned.at[me], name)
    owned[me] = projected[h, x]

    for i in (8, 9, 10):
        loads[i].wait()
    spot = lax.broadcasted_iota(jnp.int32, (LANES, own), 0)
    dense = jnp.zeros((LANES, own), f32)
    for k in range(chosen.shape[0]):
        w = jnp.broadcast_to(combine[k : k + 1, :], (LANES, own))
        e = jnp.broadcast_to(chosen[k : k + 1, :], (LANES, own))
        top = w.astype(bf16).astype(f32)
        dense = dense + jnp.where(e == spot, top, 0.0)
        dense = dense + jnp.where(e + expert_total == spot, w - top, 0.0)
    ones = lax.broadcasted_iota(jnp.int32, (own, own), 0) == lax.broadcasted_iota(
        jnp.int32, (own, own), 1
    )
    dense = lax.dot_general(
        jnp.where(ones, 1.0, 0.0).astype(bf16), dense.astype(bf16), nt, preferred_element_type=f32
    )
    gathered[h, y, x, z, :, width:] = dense.astype(bf16)

    for name in ("c", "x", "cx"):
        gh, gx = group[name]
        arrive("pr" + name, owned.at[gh * 2 + gx], name)
    attn_out = jnp.concatenate([owned[j] for j in range(4)], axis=1)
    residual = (tokens[h].astype(f32) + attn_out.astype(f32)).astype(bf16)
    gathered[h, y, x, z, :, :width] = norm(residual.astype(f32), moe_gain[...])

    def row_at(px, pz, py):
        return gathered.at[h, py, px, pz]

    def other_core(tag, ref):
        send("core" + tag, ref, ref, "c")

    def from_other(tag, px, pz, py):
        arrive("core" + tag, gathered.at[oh, py, px, pz], "c")

    plane_start("row", row_at, other_core, False)
    plane_rest("row", row_at, other_core, False)
    for k in range(4):
        zk = flip(z, k)
        from_other(f"o{k}", x, zk, y)
        from_other(f"x{k}", ox, zk, y)

    my_expert = ctx * 2 + h
    for i in (11, 12, 13):
        loads[i].wait()
    per_side = 8 * own
    tile = min(512, width)

    def run_side(side):
        tok = jnp.concatenate(
            [gathered[g, side, :, :, :, :width].reshape(per_side, width) for g in range(2)], axis=0
        )
        marks = jnp.concatenate(
            [gathered[g, side, :, :, :, width:].reshape(per_side, LANES) for g in range(2)], axis=0
        ).astype(f32)
        col = lax.broadcasted_iota(jnp.int32, (2 * per_side, LANES), 1)
        mine = (col == my_expert) | (col == my_expert + expert_total)
        weight = jnp.sum(jnp.where(mine, marks, 0.0), axis=1, keepdims=True)
        gate_part = lax.dot_general(tok, gate[...], nt, preferred_element_type=f32)
        up_part = lax.dot_general(tok, up[...], nt, preferred_element_type=f32)
        hidden = gate_part / (1.0 + jnp.exp(-gate_part)) * up_part * weight
        hidden = hidden.astype(bf16)
        for at in range(0, width, tile):
            piece = jnp.dot(hidden, down[:, at : at + tile], preferred_element_type=f32).astype(bf16)
            for g in range(2):
                partial[g, side, :, :, :, at : at + tile] = piece[
                    g * per_side : (g + 1) * per_side
                ].reshape(2, 4, own, tile)

    run_side(y)
    for q, px in (("x", ox), ("o", x)):
        send("back" + q, partial.at[oh, y, px], from_core.at[y, px], "c")
    plane_diag("row", row_at, other_core, False)
    for k in range(4):
        zk = flip(z, k)
        from_other(f"y{k}", x, zk, oy)
        from_other(f"d{k}", ox, zk, oy)
    run_side(oy)
    for q, px in (("d", ox), ("y", x)):
        send("back" + q, partial.at[oh, oy, px], from_core.at[oy, px], "c")

    def join(q, py, px):
        arrive("back" + q, from_core.at[py, px], "c")
        partial[h, py, px] = (
            partial[h, py, px].astype(f32) + from_core[py, px].astype(f32)
        ).astype(bf16)

    def diag_send(k):
        send(f"bd{k}", partial.at[h, oy, ox, flip(z, k)], from_diag.at[k], "x" if k % 2 else "y")

    def side_send(way, k, after_diag):
        py, px = (y, ox) if way == "x" else (oy, x)
        zk = flip(z, k)
        if after_diag:
            arrive(f"bd{k}", from_diag.at[k], "x" if k % 2 else "y")
            partial[h, py, px, zk] = (
                partial[h, py, px, zk].astype(f32) + from_diag[k].astype(f32)
            ).astype(bf16)
        there = from_x if way == "x" else from_y
        send(f"b{way}{k}", partial.at[h, py, px, zk], there.at[k], way)

    join("d", oy, ox)
    diag_send(3)
    diag_send(2)
    join("x", y, ox)
    side_send("x", 3, False)
    join("y", oy, x)
    side_send("y", 2, False)
    side_send("y", 3, True)
    side_send("x", 2, True)
    diag_send(1)
    diag_send(0)
    side_send("x", 1, False)
    join("o", y, x)
    side_send("y", 1, True)
    side_send("y", 0, False)
    side_send("x", 0, True)
    result = None
    for k in (3, 2, 1, 0):
        zk = flip(z, k)
        arrive(f"bx{k}", from_x.at[k], "x")
        arrive(f"by{k}", from_y.at[k], "y")
        here = partial[h, y, x, zk].astype(f32) + from_x[k].astype(f32) + from_y[k].astype(f32)
        if k:
            partial[h, y, x, zk] = here.astype(bf16)
            send(f"bz{k}", partial.at[h, y, x, zk], from_z.at[k - 1], f"z{k}")
        else:
            result = here
    for k in (1, 2, 3):
        arrive(f"bz{k}", from_z.at[k - 1], f"z{k}")
        result = result + from_z[k - 1].astype(f32)
    out[0] = (residual.astype(f32) + result).astype(bf16)
    for c in sent:
        c.wait_send()


def fused(*args):
    (
        tokens,
        attn_gain,
        wq,
        wk,
        wv,
        wo,
        moe_gain,
        chosen,
        combine,
        gate,
        up,
        down,
    ) = args
    bf16 = jnp.bfloat16
    pairs, heads, ctxs = lax.axis_size("pair"), lax.axis_size("head"), lax.axis_size("ctx")
    seqs, own, width = tokens.shape
    block = own * pairs
    span = block * ctxs
    head_dim = wk.shape[0] * pairs
    part = wq.shape[1]
    frequency = ROPE_BASE ** (-2.0 * np.arange(head_dim // 2) / head_dim)
    angles = np.arange(span)[:, None] * frequency[None, :]
    cosines, sines = np.cos(angles), np.sin(angles)
    cos_table = jnp.asarray(np.concatenate([cosines, cosines], axis=1), jnp.float32)
    sin_table = jnp.asarray(np.concatenate([-sines, sines], axis=1), jnp.float32)
    vmem = pl.BlockSpec(memory_space=pltpu.VMEM)
    anywhere = pl.BlockSpec(memory_space=pltpu.HBM)
    hidden = gate.shape[1]
    return pl.pallas_call(
        functools.partial(layer_kernel, ctxs * heads),
        out_shape=jax.ShapeDtypeStruct((1, own, width), bf16),
        in_specs=[anywhere] * 14,
        out_specs=vmem,
        scratch_shapes=[
            pltpu.VMEM(tokens.shape, bf16),
            pltpu.VMEM((1, width), jnp.float32),
            pltpu.VMEM((1, width), jnp.float32),
            pltpu.VMEM((chosen.shape[2], own), chosen.dtype),
            pltpu.VMEM((chosen.shape[2], own), jnp.float32),
            pltpu.VMEM((span, head_dim), jnp.float32),
            pltpu.VMEM((span, head_dim), jnp.float32),
            pltpu.VMEM(wq.shape, bf16),
            pltpu.VMEM(wk.shape, bf16),
            pltpu.VMEM(wv.shape, bf16),
            pltpu.VMEM(wo.shape, bf16),
            pltpu.VMEM((hidden, width), bf16),
            pltpu.VMEM((hidden, width), bf16),
            pltpu.VMEM((hidden, width), bf16),
            pltpu.VMEM((pairs, seqs, own, width), bf16),
            pltpu.VMEM((pairs, 4, 2, seqs, block, head_dim), bf16),
            pltpu.VMEM((4, seqs * block, part), bf16),
            pltpu.VMEM((seqs, pairs, own, part), bf16),
            pltpu.VMEM((4, own, part), bf16),
            pltpu.VMEM((2, 2, 2, 4, own, width + LANES), bf16),
            pltpu.VMEM((2, 2, 2, 4, own, width), bf16),
            pltpu.VMEM((2, 2, 4, own, width), bf16),
            pltpu.VMEM((4, own, width), bf16),
            pltpu.VMEM((4, own, width), bf16),
            pltpu.VMEM((4, own, width), bf16),
            pltpu.VMEM((3, own, width), bf16),
            pltpu.SemaphoreType.DMA((14,)),
            pltpu.SemaphoreType.DMA((80,)),
            pltpu.SemaphoreType.DMA((80,)),
        ],
        compiler_params=pltpu.CompilerParams(
            collective_id=0, has_side_effects=True, vmem_limit_bytes=60 * 2**20
        ),
    )(
        tokens,
        attn_gain[None],
        wq,
        wk,
        wv,
        wo,
        moe_gain[None],
        jnp.swapaxes(chosen, 1, 2),
        jnp.swapaxes(combine, 1, 2),
        gate,
        up,
        down,
        cos_table,
        sin_table,
    )


def choose(*args):
    pairs, heads, ctxs = lax.axis_size("pair"), lax.axis_size("head"), lax.axis_size("ctx")
    seqs, own, width = args[0].shape
    experts = ctxs * heads
    fits = pairs == 2 and heads == 2 and ctxs == 8 and seqs == heads
    fits = fits and 2 * experts <= LANES and args[3].shape[0] * pairs == LANES
    return fused(*args) if fits else body(*args)


def solution(mesh):
    return jax.shard_map(
        choose,
        mesh=mesh,
        in_specs=(
            P(None, ("ctx", "pair"), None),
            P(),
            P(None, ("head", "pair")),
            P(("head", "pair"), None),
            P(("head", "pair"), None),
            P(None, ("head", "pair")),
            P(),
            P("head", ("ctx", "pair"), None),
            P("head", ("ctx", "pair"), None),
            P(("ctx", "head"), "pair", None),
            P(("ctx", "head"), "pair", None),
            P(("ctx", "head"), "pair", None),
        ),
        out_specs=P("head", ("ctx", "pair"), None),
        check_vma=False,
    )
```
